128 devices in a mesh: seq: 8 (over z, core), dp: 16 (over y, x).
Axes of the slice: x: 4, y: 4, z: 4, core: 2. Of those that a mesh axis runs over, the one named last changes fastest.
Arguments:
- qkv: bfloat16 [16, 3, 1024, 16, 128], P('dp', None, 'seq'), may hold values from -14 to 14
- cotangent: bfloat16 [16, 1024, 3072], P('dp', 'seq'), may hold values from -6 to 6
- w_proj: bfloat16 [2048, 3072], replicated, may hold values from -0.125 to 0.125
- clip_levels: float32 [3072], replicated, may hold values from 0.03 to 0.3
Outputs:
- grad_qkv: bfloat16 [16, 3, 1024, 16, 128], P('dp', None, 'seq')
- d_smooth: float32 [2048], replicated
- d_clip: float32 [3072], replicated
The draws below stay inside these ranges and needn't reach their ends.
All inputs are finite; a program needn't handle non-finite values. Where the reference program divides by a largest or mean magnitude, that divisor is 1e-20 or more.
Results may differ from the reference program's by a relative error of at most 0.03.
Values may be sent and summed in bfloat16 or wider, within the bound.
No kernel may reach another device: no remote copies, remote signals or barrier semaphores. Data moves between devices by JAX's collectives and lax.ppermute only.
A program may use at most 64 MiB of HBM per device.

```python
import math
import jax
import jax.numpy as jnp
from jax import lax

D = 3072
HEADS = 16
HEAD_DIM = 128
LEN = 1024
VIDEOS = 16


def draw_qkv(key, part):
    base_key = jax.random.fold_in(key, 0)
    drawn = jax.random.truncated_normal(base_key, -4.0, 4.0, (VIDEOS, 3, LEN, HEADS, HEAD_DIM), jnp.float32)
    return drawn.astype(jnp.bfloat16)


def level_of(stream_key, shape, cuts, low, top_value):
    gain, own = 1.0, jax.random.fold_in(stream_key, 6)
    for dim, parts in cuts:
        steps = jnp.exp(jax.random.uniform(jax.random.fold_in(own, dim), (parts,), jnp.float32, low / len(cuts), top_value / len(cuts)))
        gain = gain * jnp.repeat(steps, shape[dim] // parts).reshape([-1 if axis == dim else 1 for axis in range(len(shape))])
    return gain


def scatter_about(own_key, dims, width, most, shards=(), held_as=jnp.bfloat16):
    level = level_of(own_key, dims, shards, -0.22, 0.18) if shards else 1.0
    values = jax.random.normal(own_key, dims, jnp.float32) * width * level
    return jnp.minimum(jnp.maximum(values, -most), most).astype(held_as)


def setup_inputs(seed: int = 0) -> dict:
    seeds = jax.random.split(jax.random.key(seed), 5)
    return {
        "qkv": draw_qkv(jax.random.fold_in(seeds[4], 71), 0),
        "cotangent": scatter_about(seeds[1], (VIDEOS, LEN, D), 1.0, 6.0, ((0, 16), (1, 8))),
        "w_proj": scatter_about(seeds[2], (HEADS * HEAD_DIM, D), (HEADS * HEAD_DIM) ** -0.5, 0.125),
        "clip_levels": jnp.clip(jnp.exp(jax.random.uniform(seeds[3], (D,), jnp.float32, math.log(0.03), math.log(0.3))), 0.03, 0.3),
    }


epsilon = 1e-05
act_fraction = 0.5
highest = lax.Precision.HIGHEST

def softmax_rows(queries, key_rows):
    scaling = HEAD_DIM ** (-0.5)
    scores = jnp.dot(queries, key_rows.T, precision=highest) * scaling
    row_top = lax.optimization_barrier(jnp.max(scores, axis=-1, keepdims=True))
    exponent = jnp.exp(scores - row_top)
    return exponent / lax.optimization_barrier(jnp.sum(exponent, axis=-1, keepdims=True))

def head_forward(triple):
    queries = triple[0].astype(jnp.float32)
    key_rows = triple[1].astype(jnp.float32)
    values = triple[2].astype(jnp.float32)
    weights = softmax_rows(queries, key_rows)
    weights_low = lax.optimization_barrier(weights.astype(jnp.bfloat16)).astype(jnp.float32)
    return jnp.dot(weights_low, values, precision=highest).astype(jnp.bfloat16)

def head_backward(group):
    scaling = HEAD_DIM ** (-0.5)
    queries = group[0].astype(jnp.float32)
    key_rows = group[1].astype(jnp.float32)
    values = group[2].astype(jnp.float32)
    outputs = group[3].astype(jnp.float32)
    cot_rows = group[4].astype(jnp.float32)
    weights = softmax_rows(queries, key_rows)
    weights_low = lax.optimization_barrier(weights.astype(jnp.bfloat16)).astype(jnp.float32)
    grad_weights = jnp.dot(cot_rows, values.T, precision=highest)
    row_delta = lax.optimization_barrier(jnp.sum(cot_rows * outputs, axis=-1, keepdims=True))
    grad_scores = weights * (grad_weights - row_delta)
    grad_scores = lax.optimization_barrier(grad_scores.astype(jnp.bfloat16)).astype(jnp.float32)
    grad_query = (jnp.dot(grad_scores, key_rows, precision=highest) * scaling).astype(jnp.bfloat16)
    grad_key = (jnp.dot(grad_scores.T, queries, precision=highest) * scaling).astype(jnp.bfloat16)
    grad_value = jnp.dot(weights_low.T, cot_rows, precision=highest).astype(jnp.bfloat16)
    return (grad_query, grad_key, grad_value)

def to_items(tensor):
    return tensor.transpose(0, 2, 1, 3).reshape(VIDEOS * HEADS, LEN, HEAD_DIM)

def reference(qkv, cotangent, w_proj, clip_levels):
    queries = to_items(qkv[:, 0])
    key_rows = to_items(qkv[:, 1])
    values = to_items(qkv[:, 2])
    outputs = lax.map(head_forward, (queries, key_rows, values))
    out_tokens = outputs.reshape(VIDEOS, HEADS, LEN, HEAD_DIM).transpose(0, 2, 1, 3)
    out_float = out_tokens.reshape(VIDEOS * LEN, HEADS * HEAD_DIM).astype(jnp.float32)
    act_max = lax.optimization_barrier(jnp.max(jnp.abs(out_float), axis=0))
    weight_float = w_proj.astype(jnp.float32)
    weight_max = lax.optimization_barrier(jnp.max(jnp.abs(weight_float), axis=1))
    smooth = jnp.sqrt((act_max + epsilon) / (weight_max + epsilon))
    act_clip = act_fraction * jnp.max(jnp.sqrt((act_max + epsilon) * (weight_max + epsilon)))
    smoothed = out_float / smooth
    act_tanh = jnp.tanh(smoothed / act_clip)
    act_quant = (act_clip * act_tanh).astype(jnp.bfloat16)
    ratio = smooth[:, None] * weight_float / clip_levels[None, :]
    weight_tanh = jnp.tanh(ratio)
    weight_quant = (clip_levels[None, :] * weight_tanh).astype(jnp.bfloat16)
    cot_rows = cotangent.reshape(VIDEOS * LEN, D).astype(jnp.float32)
    grad_act = jnp.dot(cot_rows, weight_quant.astype(jnp.float32).T, precision=highest)
    grad_weight = jnp.dot(act_quant.astype(jnp.float32).T, cot_rows, precision=highest)
    weight_slope = 1.0 - weight_tanh * weight_tanh
    d_clip = lax.optimization_barrier(jnp.sum(grad_weight * (weight_tanh - ratio * weight_slope), axis=0))
    grad_smoothed = grad_act * (1.0 - act_tanh * act_tanh)
    weight_part = lax.optimization_barrier(jnp.sum(grad_weight * weight_slope * weight_float, axis=1))
    act_part = lax.optimization_barrier(jnp.sum(grad_smoothed * out_float, axis=0)) / (smooth * smooth)
    d_smooth = weight_part - act_part
    grad_out = (grad_smoothed / smooth).astype(jnp.bfloat16)
    cot_items = to_items(grad_out.reshape(VIDEOS, LEN, HEADS, HEAD_DIM))
    grads = lax.map(head_backward, (queries, key_rows, values, outputs, cot_items))
    stacked = jnp.stack(grads, axis=0).reshape(3, VIDEOS, HEADS, LEN, HEAD_DIM)
    grad_qkv = stacked.transpose(1, 0, 3, 2, 4)
    return (grad_qkv, d_smooth, d_clip)
```

```python
import math

import jax
import jax.numpy as jnp
from jax import lax
from jax.experimental import pallas as pl
from jax.experimental.pallas import tpu as pltpu
from jax.sharding import PartitionSpec as P

HEADS = 16
HEAD_DIM = 128
SEQ = 8
DP = 16
LOCAL_HEADS = 2
CHANNELS = LOCAL_HEADS * HEAD_DIM
TOKENS = 128
LEN = 1024
D = 3072
BLOCK = 256
NUM_BLOCKS = LEN // BLOCK
epsilon = 1e-05
act_fraction = 0.5
SCALE = HEAD_DIM ** (-0.5)
EXP2_SCALE = SCALE * math.log2(math.e)

NN = (((1,), (0,)), ((), ()))
NT = (((1,), (1,)), ((), ()))
TN = (((0,), (0,)), ((), ()))
MIB = 1 << 20


def dot(lhs, rhs, dims):
    return lax.dot_general(lhs, rhs, dims, preferred_element_type=jnp.float32)


def to_row(column):
    return jnp.broadcast_to(column, (column.shape[0], 128)).T[0:1]


def to_column(row):
    return jnp.broadcast_to(row, (128, row.shape[1])).T[:, 0:1]


def forward_kernel(y_ref, weight_max_ref, p_ref, out_ref, message_ref):
    keys = y_ref[:, 0, 1].reshape(LEN, HEAD_DIM)
    values = y_ref[:, 0, 2].reshape(LEN, HEAD_DIM)
    top = None
    for b in range(NUM_BLOCKS):
        queries = y_ref[2 * b : 2 * b + 2, 0, 0].reshape(BLOCK, HEAD_DIM)
        scores = dot(keys, queries, NT)
        row_top = jnp.max(scores, axis=0, keepdims=True)
        exponent = jnp.exp2((scores - row_top) * EXP2_SCALE)
        total = jnp.sum(exponent, axis=0, keepdims=True)
        weights = (exponent * (1.0 / total)).astype(jnp.bfloat16)
        columns = pl.ds(b * BLOCK, BLOCK)
        p_ref[0, :, columns] = weights
        mixed = dot(values, weights, TN).astype(jnp.bfloat16)
        out_ref[0, :, columns] = mixed
        block_top = jnp.max(jnp.abs(mixed.astype(jnp.float32)), axis=1, keepdims=True)
        top = block_top if top is None else jnp.maximum(top, block_top)
    act_row = to_row(top)
    bound = jnp.max(
        jnp.sqrt((act_row + epsilon) * (weight_max_ref[0] + epsilon)), axis=1, keepdims=True
    )
    message_ref[0, 0:1] = act_row
    message_ref[0, 1:2] = jnp.broadcast_to(bound, (1, 128))


def forward(heads, weight_max):
    return pl.pallas_call(
        forward_kernel,
        grid=(LOCAL_HEADS,),
        in_specs=[
            pl.BlockSpec((SEQ, 1, 3, TOKENS, HEAD_DIM), lambda h: (0, h, 0, 0, 0)),
            pl.BlockSpec((1, 1, 128), lambda h: (h, 0, 0)),
        ],
        out_specs=[
            pl.BlockSpec((1, LEN, LEN), lambda h: (h, 0, 0)),
            pl.BlockSpec((1, HEAD_DIM, LEN), lambda h: (h, 0, 0)),
            pl.BlockSpec((1, 2, 128), lambda h: (h, 0, 0)),
        ],
        out_shape=[
            jax.ShapeDtypeStruct((LOCAL_HEADS, LEN, LEN), jnp.bfloat16),
            jax.ShapeDtypeStruct((LOCAL_HEADS, HEAD_DIM, LEN), jnp.bfloat16),
            jax.ShapeDtypeStruct((LOCAL_HEADS, 2, 128), jnp.float32),
        ],
        compiler_params=pltpu.CompilerParams(vmem_limit_bytes=28 * MIB),
        cost_estimate=pl.CostEstimate(
            flops=2 * 2 * LOCAL_HEADS * LEN * LEN * HEAD_DIM,
            bytes_accessed=6 * MIB,
            transcendentals=LOCAL_HEADS * LEN * LEN,
        ),
        name="attend_forward",
    )(heads, weight_max)


def projection_kernel(
    place_ref,
    messages_ref,
    w_ref,
    clip_ref,
    cot_ref,
    out_ref,
    grad_ref,
    quant_ref,
    part_ref,
    smooth_ref,
    wq_ref,
    scale_ref,
):
    step = pl.program_id(0)

    @pl.when(step == 0)
    def _():
        everyone = messages_ref[...]
        bound = jnp.max(everyone[:, :, 1, :], axis=0)
        bound = jnp.max(bound, axis=0, keepdims=True)
        first = pl.multiple_of(place_ref[0] * DP, DP)
        mine = messages_ref[pl.ds(first, DP)]
        act_max = jnp.max(mine[:, :, 0, :], axis=0)
        act_column = jnp.concatenate(
            [to_column(act_max[0:1]), to_column(act_max[1:2])], axis=0
        )
        weight = w_ref[...].astype(jnp.float32)
        weight_max = jnp.max(jnp.abs(weight), axis=1, keepdims=True)
        smooth = jnp.sqrt((act_column + epsilon) / (weight_max + epsilon))
        smooth_ref[...] = jnp.broadcast_to(smooth, (CHANNELS, 128))
        scale_ref[...] = jnp.broadcast_to(act_fraction * bound, (8, 128))
        clip = clip_ref[...]
        tanh = jnp.tanh((smooth * weight) * (1.0 / clip))
        wq_ref[...] = (clip * tanh).astype(jnp.bfloat16)
        part_ref[...] = jnp.zeros((CHANNELS, 128), jnp.float32)

    smooth = smooth_ref[:, 0:1]
    act_clip = scale_ref[0:1, 0:1]
    cot = cot_ref[...].reshape(BLOCK, D)
    grad_act = dot(wq_ref[...], cot, NT)
    out = out_ref[...].reshape(CHANNELS, BLOCK).astype(jnp.float32)
    inverse = 1.0 / smooth
    tanh = jnp.tanh(out * (inverse / act_clip))
    quant_ref[...] = (act_clip * tanh).astype(jnp.bfloat16)
    smoothed = grad_act * (1.0 - tanh * tanh)
    part = jnp.sum(smoothed * out, axis=1, keepdims=True) * (inverse * inverse)
    part_ref[...] += jnp.broadcast_to(part, (CHANNELS, 128))
    grad_ref[...] = (
        (smoothed * inverse).astype(jnp.bfloat16).reshape(LOCAL_HEADS, HEAD_DIM, BLOCK)
    )


def projection(place, messages, w_proj, clip, cot, out):
    return pl.pallas_call(
        projection_kernel,
        grid_spec=pltpu.PrefetchScalarGridSpec(
            num_scalar_prefetch=1,
            grid=(NUM_BLOCKS,),
            in_specs=[
                pl.BlockSpec((SEQ * DP, LOCAL_HEADS, 2, 128), lambda t, place: (0, 0, 0, 0)),
                pl.BlockSpec((CHANNELS, D), lambda t, place: (place[0], 0)),
                pl.BlockSpec((1, D), lambda t, place: (0, 0)),
                pl.BlockSpec((2, TOKENS, D), lambda t, place: (t, 0, 0)),
                pl.BlockSpec((LOCAL_HEADS, HEAD_DIM, BLOCK), lambda t, place: (0, 0, t)),
            ],
            out_specs=[
                pl.BlockSpec((LOCAL_HEADS, HEAD_DIM, BLOCK), lambda t, place: (0, 0, t)),
                pl.BlockSpec((CHANNELS, BLOCK), lambda t, place: (0, t)),
                pl.BlockSpec((CHANNELS, 128), lambda t, place: (0, 0)),
                pl.BlockSpec((CHANNELS, 128), lambda t, place: (0, 0)),
            ],
            scratch_shapes=[
                pltpu.VMEM((CHANNELS, D), jnp.bfloat16),
                pltpu.VMEM((8, 128), jnp.float32),
            ],
        ),
        out_shape=[
            jax.ShapeDtypeStruct((LOCAL_HEADS, HEAD_DIM, LEN), jnp.bfloat16),
            jax.ShapeDtypeStruct((CHANNELS, LEN), jnp.bfloat16),
            jax.ShapeDtypeStruct((CHANNELS, 128), jnp.float32),
            jax.ShapeDtypeStruct((CHANNELS, 128), jnp.float32),
        ],
        compiler_params=pltpu.CompilerParams(vmem_limit_bytes=28 * MIB),
        cost_estimate=pl.CostEstimate(
            flops=2 * CHANNELS * LEN * D, bytes_accessed=9 * MIB, transcendentals=CHANNELS * D
        ),
        name="projection_backward",
    )(place, messages, w_proj, clip, cot, out)


def backward_kernel(y_ref, p_ref, out_ref, grad_ref, z_ref, ds_ref):
    keys = y_ref[:, 0, 1].reshape(LEN, HEAD_DIM)
    values = y_ref[:, 0, 2].reshape(LEN, HEAD_DIM)
    for b in range(NUM_BLOCKS):
        columns = pl.ds(b * BLOCK, BLOCK)
        grad_out = grad_ref[0, :, columns]
        delta = jnp.sum(
            grad_out.astype(jnp.float32) * out_ref[0, :, columns].astype(jnp.float32),
            axis=0,
            keepdims=True,
        )
        grad_weights = dot(values, grad_out, NN)
        weights = p_ref[0, :, columns].astype(jnp.float32)
        grad_scores = (weights * (grad_weights - delta)).astype(jnp.bfloat16)
        ds_ref[:, columns] = grad_scores
        grad_query = dot(keys, grad_scores, TN) * SCALE
        z_ref[2 * b : 2 * b + 2, 0, 0] = (
            grad_query.T.astype(jnp.bfloat16).reshape(2, TOKENS, HEAD_DIM)
        )
    queries = y_ref[:, 0, 0].reshape(LEN, HEAD_DIM)
    grad_value = dot(p_ref[0], grad_ref[0], NT)
    z_ref[:, 0, 2] = grad_value.astype(jnp.bfloat16).reshape(SEQ, TOKENS, HEAD_DIM)
    grad_key = dot(ds_ref[...], queries, NN) * SCALE
    z_ref[:, 0, 1] = grad_key.astype(jnp.bfloat16).reshape(SEQ, TOKENS, HEAD_DIM)


def backward(heads, weights, out, grad_out):
    return pl.pallas_call(
        backward_kernel,
        grid=(LOCAL_HEADS,),
        in_specs=[
            pl.BlockSpec((SEQ, 1, 3, TOKENS, HEAD_DIM), lambda h: (0, h, 0, 0, 0)),
            pl.BlockSpec((1, LEN, LEN), lambda h: (h, 0, 0)),
            pl.BlockSpec((1, HEAD_DIM, LEN), lambda h: (h, 0, 0)),
            pl.BlockSpec((1, HEAD_DIM, LEN), lambda h: (h, 0, 0)),
        ],
        out_specs=pl.BlockSpec((SEQ, 1, 3, TOKENS, HEAD_DIM), lambda h: (0, h, 0, 0, 0)),
        out_shape=jax.ShapeDtypeStruct(
            (SEQ, LOCAL_HEADS, 3, TOKENS, HEAD_DIM), jnp.bfloat16
        ),
        scratch_shapes=[pltpu.VMEM((LEN, LEN), jnp.bfloat16)],
        compiler_params=pltpu.CompilerParams(vmem_limit_bytes=28 * MIB),
        cost_estimate=pl.CostEstimate(
            flops=4 * 2 * LOCAL_HEADS * LEN * LEN * HEAD_DIM,
            bytes_accessed=8 * MIB,
            transcendentals=0,
        ),
        name="attend_backward",
    )(heads, weights, out, grad_out)


WIDTH = 512


def weight_kernel(place_ref, w_ref, clip_ref, cot_ref, quant_ref, part_ref, smooth_ref, vec_ref, acc_ref):
    step = pl.program_id(0)
    smooth = smooth_ref[:, 0:1]

    @pl.when(step == 0)
    def _():
        vec_ref[...] = jnp.zeros_like(vec_ref)
        acc_ref[...] = -part_ref[...]

    weight = w_ref[...].astype(jnp.float32)
    grad_weight = dot(quant_ref[...], cot_ref[...].reshape(LEN, WIDTH), NN)
    ratio = (smooth * weight) * (1.0 / clip_ref[...])
    tanh = jnp.tanh(ratio)
    slope = 1.0 - tanh * tanh
    clip_part = jnp.sum(grad_weight * (tanh - ratio * slope), axis=0, keepdims=True)
    column = pl.multiple_of(HEADS * HEAD_DIM + step * WIDTH, WIDTH)
    vec_ref[:, pl.ds(column, WIDTH)] = clip_part
    smooth_part = jnp.sum(grad_weight * slope * weight, axis=1, keepdims=True)
    acc_ref[...] += jnp.broadcast_to(smooth_part, (CHANNELS, 128))

    @pl.when(step == D // WIDTH - 1)
    def _():
        row = acc_ref[...].T[0:1]
        first = pl.multiple_of(place_ref[0] * CHANNELS, CHANNELS)
        vec_ref[:, pl.ds(first, CHANNELS)] = row


def weight_side(place, w_proj, clip, cot, quant, part, smooth):
    return pl.pallas_call(
        weight_kernel,
        grid_spec=pltpu.PrefetchScalarGridSpec(
            num_scalar_prefetch=1,
            grid=(D // WIDTH,),
            in_specs=[
                pl.BlockSpec((CHANNELS, WIDTH), lambda j, place: (place[0], j)),
                pl.BlockSpec((1, WIDTH), lambda j, place: (0, j)),
                pl.BlockSpec((SEQ, TOKENS, WIDTH), lambda j, place: (0, 0, j)),
                pl.BlockSpec((CHANNELS, LEN), lambda j, place: (0, 0)),
                pl.BlockSpec((CHANNELS, 128), lambda j, place: (0, 0)),
                pl.BlockSpec((CHANNELS, 128), lambda j, place: (0, 0)),
            ],
            out_specs=pl.BlockSpec((1, HEADS * HEAD_DIM + D), lambda j, place: (0, 0)),
            scratch_shapes=[pltpu.VMEM((CHANNELS, 128), jnp.float32)],
        ),
        out_shape=jax.ShapeDtypeStruct((1, HEADS * HEAD_DIM + D), jnp.float32),
        compiler_params=pltpu.CompilerParams(vmem_limit_bytes=28 * MIB),
        cost_estimate=pl.CostEstimate(
            flops=2 * CHANNELS * LEN * D, bytes_accessed=9 * MIB, transcendentals=CHANNELS * D
        ),
        name="weight_side",
    )(place, w_proj, clip, cot, quant, part, smooth)


def total_over_devices(vector):
    for axis, size, bit in (
        ("seq", SEQ, 1),
        ("seq", SEQ, 2),
        ("seq", SEQ, 4),
        ("dp", DP, 1),
        ("dp", DP, 2),
        ("dp", DP, 4),
        ("dp", DP, 8),
    ):
        pairs = [(i, i ^ bit) for i in range(size)]
        vector = vector + lax.ppermute(vector, axis, pairs)
    return vector


def per_device(qkv, cotangent, w_proj, clip_levels):
    place = lax.axis_index("seq")
    place_vector = place.astype(jnp.int32).reshape(1)
    clip = clip_levels.reshape(1, D)
    cot = lax.all_gather(cotangent[0], "seq")
    send = qkv[0].reshape(3, TOKENS, SEQ, LOCAL_HEADS, HEAD_DIM).transpose(2, 3, 0, 1, 4)
    heads = lax.all_to_all(send, "seq", split_axis=0, concat_axis=0, tiled=True)
    own_rows = lax.dynamic_slice_in_dim(w_proj, place * CHANNELS, CHANNELS, axis=0)
    weight_max = jnp.max(jnp.abs(own_rows), axis=1).astype(jnp.float32)
    weights, out, message = forward(heads, weight_max.reshape(LOCAL_HEADS, 1, 128))
    messages = lax.all_to_all(
        jnp.broadcast_to(message[None], (SEQ * DP, LOCAL_HEADS, 2, 128)),
        ("seq", "dp"),
        split_axis=0,
        concat_axis=0,
        tiled=True,
    )
    grad_out, quant, part, smooth = projection(
        place_vector, messages, w_proj, clip, cot, out
    )
    back = backward(heads, weights, out, grad_out)
    back, quant = lax.optimization_barrier((back, quant))
    received = lax.all_to_all(back, "seq", split_axis=0, concat_axis=0, tiled=True)
    vector = weight_side(place_vector, w_proj, clip, cot, quant, part, smooth)
    vector = total_over_devices(vector)[0]
    grad_qkv = received.transpose(2, 3, 0, 1, 4).reshape(1, 3, TOKENS, HEADS, HEAD_DIM)
    return (grad_qkv, vector[: HEADS * HEAD_DIM], vector[HEADS * HEAD_DIM :])


def solution(mesh):
    in_specs = (P("dp", None, "seq", None, None), P("dp", "seq", None), P(), P())
    out_specs = (P("dp", None, "seq", None, None), P(), P())
    return jax.shard_map(
        per_device, mesh=mesh, in_specs=in_specs, out_specs=out_specs, check_vma=False
    )
```

```python
import math

import jax
import jax.numpy as jnp
from jax import lax
from jax.experimental import pallas as pl
from jax.experimental.pallas import tpu as pltpu
from jax.sharding import PartitionSpec as P

HEADS = 16
HEAD_DIM = 128
SEQ = 8
DP = 16
LOCAL_HEADS = 2
CHANNELS = LOCAL_HEADS * HEAD_DIM
TOKENS = 128
LEN = 1024
D = 3072
BLOCK = 256
NUM_BLOCKS = LEN // BLOCK
epsilon = 1e-05
act_fraction = 0.5
SCALE = HEAD_DIM ** (-0.5)
EXP2_SCALE = SCALE * math.log2(math.e)

NN = (((1,), (0,)), ((), ()))
NT = (((1,), (1,)), ((), ()))
TN = (((0,), (0,)), ((), ()))
MIB = 1 << 20
VMEM_LIMIT = 24 * MIB


def dot(lhs, rhs, dims):
    return lax.dot_general(lhs, rhs, dims, preferred_element_type=jnp.float32)


def to_row(column):
    return jnp.broadcast_to(column, (column.shape[0], 128)).T[0:1]


def to_column(row):
    return jnp.broadcast_to(row, (128, row.shape[1])).T[:, 0:1]


def forward_kernel(y_ref, weight_max_ref, p_ref, out_ref, message_ref):
    keys = y_ref[:, 0, 1].reshape(LEN, HEAD_DIM)
    values = y_ref[:, 0, 2].reshape(LEN, HEAD_DIM)
    top = None
    for b in range(NUM_BLOCKS):
        queries = y_ref[2 * b : 2 * b + 2, 0, 0].reshape(BLOCK, HEAD_DIM)
        scores = dot(keys, queries, NT)
        row_top = jnp.max(scores, axis=0, keepdims=True)
        exponent = jnp.exp2((scores - row_top) * EXP2_SCALE)
        total = jnp.sum(exponent, axis=0, keepdims=True)
        weights = (exponent * (1.0 / total)).astype(jnp.bfloat16)
        columns = pl.ds(b * BLOCK, BLOCK)
        p_ref[0, :, columns] = weights
        mixed = dot(values, weights, TN).astype(jnp.bfloat16)
        out_ref[0, :, columns] = mixed
        block_top = jnp.max(jnp.abs(mixed.astype(jnp.float32)), axis=1, keepdims=True)
        top = block_top if top is None else jnp.maximum(top, block_top)
    act_row = to_row(top)
    bound = jnp.max(
        jnp.sqrt((act_row + epsilon) * (weight_max_ref[0] + epsilon)), axis=1, keepdims=True
    )
    message_ref[0, 0:1] = act_row
    message_ref[0, 1:2] = jnp.broadcast_to(bound, (1, 128))


def forward(heads, weight_max):
    return pl.pallas_call(
        forward_kernel,
        grid=(LOCAL_HEADS,),
        in_specs=[
            pl.BlockSpec((SEQ, 1, 3, TOKENS, HEAD_DIM), lambda h: (0, h, 0, 0, 0)),
            pl.BlockSpec((1, 1, 128), lambda h: (h, 0, 0)),
        ],
        out_specs=[
            pl.BlockSpec((1, LEN, LEN), lambda h: (h, 0, 0)),
            pl.BlockSpec((1, HEAD_DIM, LEN), lambda h: (h, 0, 0)),
            pl.BlockSpec((1, 2, 128), lambda h: (h, 0, 0)),
        ],
        out_shape=[
            jax.ShapeDtypeStruct((LOCAL_HEADS, LEN, LEN), jnp.bfloat16),
            jax.ShapeDtypeStruct((LOCAL_HEADS, HEAD_DIM, LEN), jnp.bfloat16),
            jax.ShapeDtypeStruct((LOCAL_HEADS, 2, 128), jnp.float32),
        ],
        compiler_params=pltpu.CompilerParams(vmem_limit_bytes=VMEM_LIMIT),
        cost_estimate=pl.CostEstimate(
            flops=2 * 2 * LOCAL_HEADS * LEN * LEN * HEAD_DIM,
            bytes_accessed=6 * MIB,
            transcendentals=LOCAL_HEADS * LEN * LEN,
        ),
        name="attend_forward",
    )(heads, weight_max)


HALF = TOKENS // 2
WIDTH = 512


def projection_kernel(place_ref, messages_ref, clip_ref, out_ref, own_ref, *rest):
    pieces = rest[:10]
    grad_ref, vec_ref, cot_ref, wq_ref, tanh_ref, quant_ref, sem = rest[10:]
    place = place_ref[0]
    depth = place // 2
    core = place % 2
    copies = []
    for k, piece in enumerate(pieces):
        kind, sibling = k % 5, k // 5
        rows = TOKENS if kind < 3 else HALF
        source = (depth + (0, 3, 1, 2, 2)[kind]) % 4
        first = (source * 2 + (core + sibling) % 2) * TOKENS + (HALF if kind == 4 else 0)
        copy = pltpu.make_async_copy(
            piece, cot_ref.at[pl.ds(pl.multiple_of(first, HALF), rows)], sem.at[k]
        )
        copy.start()
        copies.append(copy)
    bound = jnp.max(messages_ref[:, :, 1, :], axis=0)
    bound = jnp.max(jnp.max(bound, axis=0, keepdims=True), axis=1, keepdims=True)
    act_clip = act_fraction * bound
    mine = messages_ref[pl.ds(pl.multiple_of(place * DP, DP), DP)]
    act_max = jnp.max(mine[:, :, 0, :], axis=0)
    act_column = jnp.concatenate([to_column(act_max[0:1]), to_column(act_max[1:2])], axis=0)
    weight_max = None
    for j in range(D // WIDTH):
        weight = own_ref[:, j * WIDTH : (j + 1) * WIDTH]
        top = jnp.max(jnp.abs(weight.astype(jnp.float32)), axis=1, keepdims=True)
        weight_max = top if weight_max is None else jnp.maximum(weight_max, top)
    smooth = jnp.sqrt((act_column + epsilon) / (weight_max + epsilon))
    for j in range(D // WIDTH):
        columns = slice(j * WIDTH, (j + 1) * WIDTH)
        clip = clip_ref[:, columns]
        weight = own_ref[:, columns].astype(jnp.float32)
        tanh = jnp.tanh((smooth * weight) * (1.0 / clip))
        tanh_ref[:, columns] = tanh
        wq_ref[:, columns] = (clip * tanh).astype(jnp.bfloat16)
    inverse = 1.0 / smooth
    inner = inverse / act_clip
    for copy in copies:
        copy.wait()
    act_part = None
    for t in range(NUM_BLOCKS):
        tokens = slice(t * BLOCK, (t + 1) * BLOCK)
        grad_act = dot(wq_ref[...], cot_ref[tokens], NT)
        out = out_ref[:, :, tokens].reshape(CHANNELS, BLOCK).astype(jnp.float32)
        tanh = jnp.tanh(out * inner)
        quant_ref[:, tokens] = (act_clip * tanh).astype(jnp.bfloat16)
        smoothed = grad_act * (1.0 - tanh * tanh)
        part = jnp.sum(smoothed * out, axis=1, keepdims=True)
        act_part = part if act_part is None else act_part + part
        grad_ref[:, :, tokens] = (
            (smoothed * inverse).astype(jnp.bfloat16).reshape(LOCAL_HEADS, HEAD_DIM, BLOCK)
        )
    smooth_part = -act_part * (inverse * inverse)
    vec_ref[...] = jnp.zeros_like(vec_ref)
    for j in range(D // WIDTH):
        columns = slice(j * WIDTH, (j + 1) * WIDTH)
        weight = own_ref[:, columns].astype(jnp.float32)
        grad_weight = dot(quant_ref[...], cot_ref[:, columns], NN)
        ratio = (smooth * weight) * (1.0 / clip_ref[:, columns])
        tanh = tanh_ref[:, columns]
        slope = 1.0 - tanh * tanh
        vec_ref[:, HEADS * HEAD_DIM + j * WIDTH : HEADS * HEAD_DIM + (j + 1) * WIDTH] = jnp.sum(
            grad_weight * (tanh - ratio * slope), axis=0, keepdims=True
        )
        smooth_part += jnp.sum(grad_weight * slope * weight, axis=1, keepdims=True)
    vec_ref[:, pl.ds(pl.multiple_of(place * CHANNELS, CHANNELS), CHANNELS)] = to_row(smooth_part)


def projection(place, messages, clip, out, own_rows, pieces):
    vmem = pl.BlockSpec(memory_space=pltpu.VMEM)
    hbm = pl.BlockSpec(memory_space=pl.ANY)
    return pl.pallas_call(
        projection_kernel,
        in_specs=[pl.BlockSpec(memory_space=pltpu.SMEM), vmem, vmem, vmem, vmem] + [hbm] * 10,
        out_specs=[vmem, vmem],
        out_shape=[
            jax.ShapeDtypeStruct((LOCAL_HEADS, HEAD_DIM, LEN), jnp.bfloat16),
            jax.ShapeDtypeStruct((1, HEADS * HEAD_DIM + D), jnp.float32),
        ],
        scratch_shapes=[
            pltpu.VMEM((LEN, D), jnp.bfloat16),
            pltpu.VMEM((CHANNELS, D), jnp.bfloat16),
            pltpu.VMEM((CHANNELS, D), jnp.float32),
            pltpu.VMEM((CHANNELS, LEN), jnp.bfloat16),
            pltpu.SemaphoreType.DMA((10,)),
        ],
        compiler_params=pltpu.CompilerParams(vmem_limit_bytes=VMEM_LIMIT),
        cost_estimate=pl.CostEstimate(
            flops=2 * 2 * CHANNELS * LEN * D,
            bytes_accessed=9 * MIB,
            transcendentals=CHANNELS * (D + LEN),
        ),
        name="projection_backward",
    )(place, messages, clip, out, own_rows, *pieces)


def backward_kernel(y_ref, p_ref, out_ref, grad_ref, z_ref, ds_ref):
    keys = y_ref[:, 0, 1].reshape(LEN, HEAD_DIM)
    values = y_ref[:, 0, 2].reshape(LEN, HEAD_DIM)
    for b in range(NUM_BLOCKS):
        columns = pl.ds(b * BLOCK, BLOCK)
        grad_out = grad_ref[0, :, columns]
        delta = jnp.sum(
            grad_out.astype(jnp.float32) * out_ref[0, :, columns].astype(jnp.float32),
            axis=0,
            keepdims=True,
        )
        grad_weights = dot(values, grad_out, NN)
        weights = p_ref[0, :, columns].astype(jnp.float32)
        grad_scores = (weights * (grad_weights - delta)).astype(jnp.bfloat16)
        ds_ref[:, columns] = grad_scores
        grad_query = dot(keys, grad_scores, TN) * SCALE
        z_ref[2 * b : 2 * b + 2, 0, 0] = (
            grad_query.T.astype(jnp.bfloat16).reshape(2, TOKENS, HEAD_DIM)
        )
    queries = y_ref[:, 0, 0].reshape(LEN, HEAD_DIM)
    grad_value = dot(p_ref[0], grad_ref[0], NT)
    z_ref[:, 0, 2] = grad_value.astype(jnp.bfloat16).reshape(SEQ, TOKENS, HEAD_DIM)
    grad_key = dot(ds_ref[...], queries, NN) * SCALE
    z_ref[:, 0, 1] = grad_key.astype(jnp.bfloat16).reshape(SEQ, TOKENS, HEAD_DIM)


def backward(heads, weights, out, grad_out):
    return pl.pallas_call(
        backward_kernel,
        grid=(LOCAL_HEADS,),
        in_specs=[
            pl.BlockSpec((SEQ, 1, 3, TOKENS, HEAD_DIM), lambda h: (0, h, 0, 0, 0)),
            pl.BlockSpec((1, LEN, LEN), lambda h: (h, 0, 0)),
            pl.BlockSpec((1, HEAD_DIM, LEN), lambda h: (h, 0, 0)),
            pl.BlockSpec((1, HEAD_DIM, LEN), lambda h: (h, 0, 0)),
        ],
        out_specs=pl.BlockSpec((SEQ, 1, 3, TOKENS, HEAD_DIM), lambda h: (0, h, 0, 0, 0)),
        out_shape=jax.ShapeDtypeStruct(
            (SEQ, LOCAL_HEADS, 3, TOKENS, HEAD_DIM), jnp.bfloat16
        ),
        scratch_shapes=[pltpu.VMEM((LEN, LEN), jnp.bfloat16)],
        compiler_params=pltpu.CompilerParams(vmem_limit_bytes=VMEM_LIMIT),
        cost_estimate=pl.CostEstimate(
            flops=4 * 2 * LOCAL_HEADS * LEN * LEN * HEAD_DIM,
            bytes_accessed=8 * MIB,
            transcendentals=0,
        ),
        name="attend_backward",
    )(heads, weights, out, grad_out)


def total_over_depth(vector):
    moved = [
        lax.ppermute(vector, "seq", [(i, i ^ bits) for i in range(SEQ)]) for bits in (2, 4, 6)
    ]
    return (vector + moved[0]) + (moved[1] + moved[2])


def total_over_rest(vector):
    for axis, size, bit in (
        ("dp", DP, 1),
        ("dp", DP, 2),
        ("dp", DP, 4),
        ("dp", DP, 8),
        ("seq", SEQ, 1),
    ):
        vector = vector + lax.ppermute(vector, axis, [(i, i ^ bit) for i in range(size)])
    return vector


def shift_depth(tensor, steps):
    return lax.ppermute(tensor, "seq", [(i, (i + 2 * steps) % SEQ) for i in range(SEQ)])


def swap_cores(tensor):
    return lax.ppermute(tensor, "seq", [(i, i ^ 1) for i in range(SEQ)])


def after(tensors, *earlier):
    return lax.optimization_barrier((tensors, earlier))[0]


def per_device(qkv, cotangent, w_proj, clip_levels):
    place = lax.axis_index("seq")
    place_vector = place.astype(jnp.int32).reshape(1)
    clip = clip_levels.reshape(1, D)
    own = cotangent[0]
    own_rows = lax.optimization_barrier(
        lax.dynamic_slice_in_dim(w_proj, place * CHANNELS, CHANNELS, axis=0)
    )
    send = qkv[0].reshape(3, TOKENS, SEQ, LOCAL_HEADS, HEAD_DIM).transpose(2, 3, 0, 1, 4)
    heads = lax.all_to_all(send, "seq", split_axis=0, concat_axis=0, tiled=True)
    weight_max = jnp.max(jnp.abs(own_rows), axis=1).astype(jnp.float32)
    weight_max = weight_max.reshape(LOCAL_HEADS, 1, 128)
    own_swapped = swap_cores(own)
    own_1, weight_max = after((own, weight_max), heads)
    before = shift_depth(own_1, 1)
    behind = shift_depth(own_1, -1)
    weights, out, message = forward(heads, weight_max)
    messages = lax.all_to_all(
        jnp.broadcast_to(message[None], (SEQ * DP, LOCAL_HEADS, 2, 128)),
        ("seq", "dp"),
        split_axis=0,
        concat_axis=0,
        tiled=True,
    )
    before, behind = after((before, behind), message)
    far_low = shift_depth(before[:HALF], 1)
    far_high = shift_depth(behind[HALF:], -1)
    pieces = [own, before, behind, far_low, far_high, own_swapped]
    pieces += [swap_cores(piece) for piece in (before, behind)]
    pieces += [swap_cores(piece) for piece in after((far_low, far_high), messages)]
    grad_out, vector = projection(place_vector, messages, clip, out, own_rows, pieces)
    back = backward(heads, weights, out, grad_out)
    back, vector = lax.optimization_barrier((back, total_over_depth(vector)))
    received = lax.all_to_all(back, "seq", split_axis=0, concat_axis=0, tiled=True)
    vector = total_over_rest(vector)[0]
    grad_qkv = received.transpose(2, 3, 0, 1, 4).reshape(1, 3, TOKENS, HEADS, HEAD_DIM)
    return (grad_qkv, vector[: HEADS * HEAD_DIM], vector[HEADS * HEAD_DIM :])


def solution(mesh):
    in_specs = (P("dp", None, "seq", None, None), P("dp", "seq", None), P(), P())
    out_specs = (P("dp", None, "seq", None, None), P(), P())
    return jax.shard_map(
        per_device, mesh=mesh, in_specs=in_specs, out_specs=out_specs, check_vma=False
    )
```

```python
import math

import jax
import jax.numpy as jnp
from jax import lax
from jax.experimental import pallas as pl
from jax.experimental.pallas import tpu as pltpu
from jax.sharding import PartitionSpec as P

HEADS = 16
HEAD_DIM = 128
SEQ = 8
DP = 16
LOCAL_HEADS = 2
CHANNELS = LOCAL_HEADS * HEAD_DIM
TOKENS = 128
LEN = 1024
D = 3072
BLOCK = 256
NUM_BLOCKS = LEN // BLOCK
epsilon = 1e-05
act_fraction = 0.5
SCALE = HEAD_DIM ** (-0.5)
EXP2_SCALE = SCALE * math.log2(math.e)

NN = (((1,), (0,)), ((), ()))
NT = (((1,), (1,)), ((), ()))
TN = (((0,), (0,)), ((), ()))
MIB = 1 << 20
VMEM_LIMIT = 24 * MIB


def dot(lhs, rhs, dims):
    return lax.dot_general(lhs, rhs, dims, preferred_element_type=jnp.float32)


def to_row(column):
    return jnp.broadcast_to(column, (column.shape[0], 128)).T[0:1]


def to_column(row):
    return jnp.broadcast_to(row, (128, row.shape[1])).T[:, 0:1]


def forward_kernel(y_ref, weight_max_ref, p_ref, out_ref, message_ref):
    keys = y_ref[:, 0, 1].reshape(LEN, HEAD_DIM)
    values = y_ref[:, 0, 2].reshape(LEN, HEAD_DIM)
    top = None
    for b in range(NUM_BLOCKS):
        queries = y_ref[2 * b : 2 * b + 2, 0, 0].reshape(BLOCK, HEAD_DIM)
        scores = dot(keys, queries, NT)
        row_top = jnp.max(scores, axis=0, keepdims=True)
        exponent = jnp.exp2((scores - row_top) * EXP2_SCALE)
        total = jnp.sum(exponent, axis=0, keepdims=True)
        weights = (exponent * (1.0 / total)).astype(jnp.bfloat16)
        columns = pl.ds(b * BLOCK, BLOCK)
        p_ref[0, :, columns] = weights
        mixed = dot(values, weights, TN).astype(jnp.bfloat16)
        out_ref[0, :, columns] = mixed
        block_top = jnp.max(jnp.abs(mixed.astype(jnp.float32)), axis=1, keepdims=True)
        top = block_top if top is None else jnp.maximum(top, block_top)
    act_row = to_row(top)
    bound = jnp.max(
        jnp.sqrt((act_row + epsilon) * (weight_max_ref[0] + epsilon)), axis=1, keepdims=True
    )
    head = pl.program_id(0)

    @pl.when(head == 0)
    def _():
        message_ref[...] = jnp.zeros_like(message_ref)

    message_ref[pl.ds(head, 1)] = act_row
    message_ref[2:3] = jnp.maximum(message_ref[2:3], bound)


def forward(heads, weight_max):
    return pl.pallas_call(
        forward_kernel,
        grid=(LOCAL_HEADS,),
        in_specs=[
            pl.BlockSpec((SEQ, 1, 3, TOKENS, HEAD_DIM), lambda h: (0, h, 0, 0, 0)),
            pl.BlockSpec((1, 1, 128), lambda h: (h, 0, 0)),
        ],
        out_specs=[
            pl.BlockSpec((1, LEN, LEN), lambda h: (h, 0, 0)),
            pl.BlockSpec((1, HEAD_DIM, LEN), lambda h: (h, 0, 0)),
            pl.BlockSpec((8, 128), lambda h: (0, 0)),
        ],
        out_shape=[
            jax.ShapeDtypeStruct((LOCAL_HEADS, LEN, LEN), jnp.bfloat16),
            jax.ShapeDtypeStruct((LOCAL_HEADS, HEAD_DIM, LEN), jnp.bfloat16),
            jax.ShapeDtypeStruct((8, 128), jnp.float32),
        ],
        compiler_params=pltpu.CompilerParams(vmem_limit_bytes=VMEM_LIMIT),
        cost_estimate=pl.CostEstimate(
            flops=2 * 2 * LOCAL_HEADS * LEN * LEN * HEAD_DIM,
            bytes_accessed=6 * MIB,
            transcendentals=LOCAL_HEADS * LEN * LEN,
        ),
        name="attend_forward",
    )(heads, weight_max)


HALF = TOKENS // 2
WIDTH = 512


def projection_kernel(place_ref, message_ref, bound_ref, clip_ref, out_ref, own_ref, *rest):
    pieces = rest[:10]
    grad_ref, vec_ref, cot_ref, wq_ref, tanh_ref, quant_ref, sem = rest[10:]
    place = place_ref[0]
    depth = place // 2
    core = place % 2
    copies = []
    for k, piece in enumerate(pieces):
        kind, sibling = k % 5, k // 5
        rows = TOKENS if kind < 3 else HALF
        source = (depth + (0, 3, 1, 2, 2)[kind]) % 4
        first = (source * 2 + (core + sibling) % 2) * TOKENS + (HALF if kind == 4 else 0)
        copy = pltpu.make_async_copy(
            piece, cot_ref.at[pl.ds(pl.multiple_of(first, HALF), rows)], sem.at[k]
        )
        copy.start()
        copies.append(copy)
    act_clip = act_fraction * bound_ref[2:3, 0:1]
    act_column = jnp.concatenate(
        [to_column(message_ref[0:1]), to_column(message_ref[1:2])], axis=0
    )
    weight_max = None
    for j in range(D // WIDTH):
        weight = own_ref[:, j * WIDTH : (j + 1) * WIDTH]
        top = jnp.max(jnp.abs(weight.astype(jnp.float32)), axis=1, keepdims=True)
        weight_max = top if weight_max is None else jnp.maximum(weight_max, top)
    smooth = jnp.sqrt((act_column + epsilon) / (weight_max + epsilon))
    for j in range(D // WIDTH):
        columns = slice(j * WIDTH, (j + 1) * WIDTH)
        clip = clip_ref[:, columns]
        weight = own_ref[:, columns].astype(jnp.float32)
        tanh = jnp.tanh((smooth * weight) * (1.0 / clip))
        tanh_ref[:, columns] = tanh
        wq_ref[:, columns] = (clip * tanh).astype(jnp.bfloat16)
    inverse = 1.0 / smooth
    inner = inverse / act_clip
    for copy in copies:
        copy.wait()
    act_part = None
    for t in range(NUM_BLOCKS):
        tokens = slice(t * BLOCK, (t + 1) * BLOCK)
        grad_act = dot(wq_ref[...], cot_ref[tokens], NT)
        out = out_ref[:, :, tokens].reshape(CHANNELS, BLOCK).astype(jnp.float32)
        tanh = jnp.tanh(out * inner)
        quant_ref[:, tokens] = (act_clip * tanh).astype(jnp.bfloat16)
        smoothed = grad_act * (1.0 - tanh * tanh)
        part = jnp.sum(smoothed * out, axis=1, keepdims=True)
        act_part = part if act_part is None else act_part + part
        grad_ref[:, :, tokens] = (
            (smoothed * inverse).astype(jnp.bfloat16).reshape(LOCAL_HEADS, HEAD_DIM, BLOCK)
        )
    smooth_part = -act_part * (inverse * inverse)
    vec_ref[...] = jnp.zeros_like(vec_ref)
    for j in range(D // WIDTH):
        columns = slice(j * WIDTH, (j + 1) * WIDTH)
        weight = own_ref[:, columns].astype(jnp.float32)
        grad_weight = dot(quant_ref[...], cot_ref[:, columns], NN)
        ratio = (smooth * weight) * (1.0 / clip_ref[:, columns])
        tanh = tanh_ref[:, columns]
        slope = 1.0 - tanh * tanh
        vec_ref[:, HEADS * HEAD_DIM + j * WIDTH : HEADS * HEAD_DIM + (j + 1) * WIDTH] = jnp.sum(
            grad_weight * (tanh - ratio * slope), axis=0, keepdims=True
        )
        smooth_part += jnp.sum(grad_weight * slope * weight, axis=1, keepdims=True)
    vec_ref[:, pl.ds(pl.multiple_of(place * CHANNELS, CHANNELS), CHANNELS)] = to_row(smooth_part)


def projection(place, message, bound, clip, out, own_rows, pieces):
    vmem = pl.BlockSpec(memory_space=pltpu.VMEM)
    hbm = pl.BlockSpec(memory_space=pl.ANY)
    return pl.pallas_call(
        projection_kernel,
        in_specs=[pl.BlockSpec(memory_space=pltpu.SMEM), vmem, vmem, vmem, vmem, vmem] + [hbm] * 10,
        out_specs=[vmem, vmem],
        out_shape=[
            jax.ShapeDtypeStruct((LOCAL_HEADS, HEAD_DIM, LEN), jnp.bfloat16),
            jax.ShapeDtypeStruct((1, HEADS * HEAD_DIM + D), jnp.float32),
        ],
        scratch_shapes=[
            pltpu.VMEM((LEN, D), jnp.bfloat16),
            pltpu.VMEM((CHANNELS, D), jnp.bfloat16),
            pltpu.VMEM((CHANNELS, D), jnp.float32),
            pltpu.VMEM((CHANNELS, LEN), jnp.bfloat16),
            pltpu.SemaphoreType.DMA((10,)),
        ],
        compiler_params=pltpu.CompilerParams(vmem_limit_bytes=VMEM_LIMIT),
        cost_estimate=pl.CostEstimate(
            flops=2 * 2 * CHANNELS * LEN * D,
            bytes_accessed=9 * MIB,
            transcendentals=CHANNELS * (D + LEN),
        ),
        name="projection_backward",
    )(place, message, bound, clip, out, own_rows, *pieces)


def backward_kernel(y_ref, p_ref, out_ref, grad_ref, z_ref, ds_ref):
    keys = y_ref[:, 0, 1].reshape(LEN, HEAD_DIM)
    values = y_ref[:, 0, 2].reshape(LEN, HEAD_DIM)
    for b in range(NUM_BLOCKS):
        columns = pl.ds(b * BLOCK, BLOCK)
        grad_out = grad_ref[0, :, columns]
        delta = jnp.sum(
            grad_out.astype(jnp.float32) * out_ref[0, :, columns].astype(jnp.float32),
            axis=0,
            keepdims=True,
        )
        grad_weights = dot(values, grad_out, NN)
        weights = p_ref[0, :, columns].astype(jnp.float32)
        grad_scores = (weights * (grad_weights - delta)).astype(jnp.bfloat16)
        ds_ref[:, columns] = grad_scores
        grad_query = dot(keys, grad_scores, TN) * SCALE
        z_ref[2 * b : 2 * b + 2, 0, 0] = (
            grad_query.T.astype(jnp.bfloat16).reshape(2, TOKENS, HEAD_DIM)
        )
    queries = y_ref[:, 0, 0].reshape(LEN, HEAD_DIM)
    grad_value = dot(p_ref[0], grad_ref[0], NT)
    z_ref[:, 0, 2] = grad_value.astype(jnp.bfloat16).reshape(SEQ, TOKENS, HEAD_DIM)
    grad_key = dot(ds_ref[...], queries, NN) * SCALE
    z_ref[:, 0, 1] = grad_key.astype(jnp.bfloat16).reshape(SEQ, TOKENS, HEAD_DIM)


def backward(heads, weights, out, grad_out):
    return pl.pallas_call(
        backward_kernel,
        grid=(LOCAL_HEADS,),
        in_specs=[
            pl.BlockSpec((SEQ, 1, 3, TOKENS, HEAD_DIM), lambda h: (0, h, 0, 0, 0)),
            pl.BlockSpec((1, LEN, LEN), lambda h: (h, 0, 0)),
            pl.BlockSpec((1, HEAD_DIM, LEN), lambda h: (h, 0, 0)),
            pl.BlockSpec((1, HEAD_DIM, LEN), lambda h: (h, 0, 0)),
        ],
        out_specs=pl.BlockSpec((SEQ, 1, 3, TOKENS, HEAD_DIM), lambda h: (0, h, 0, 0, 0)),
        out_shape=jax.ShapeDtypeStruct(
            (SEQ, LOCAL_HEADS, 3, TOKENS, HEAD_DIM), jnp.bfloat16
        ),
        scratch_shapes=[pltpu.VMEM((LEN, LEN), jnp.bfloat16)],
        compiler_params=pltpu.CompilerParams(vmem_limit_bytes=VMEM_LIMIT),
        cost_estimate=pl.CostEstimate(
            flops=4 * 2 * LOCAL_HEADS * LEN * LEN * HEAD_DIM,
            bytes_accessed=8 * MIB,
            transcendentals=0,
        ),
        name="attend_backward",
    )(heads, weights, out, grad_out)


def exchange(tensor, axis, size, bits):
    return lax.ppermute(tensor, axis, [(i, i ^ bits) for i in range(size)])


def total_over_depth(vector):
    moved = [exchange(vector, "seq", SEQ, bits) for bits in (2, 4, 6)]
    return (vector + moved[0]) + (moved[1] + moved[2])


def total_over_rest(vector):
    for axis, size, bit in (
        ("dp", DP, 1),
        ("dp", DP, 2),
        ("dp", DP, 4),
        ("dp", DP, 8),
        ("seq", SEQ, 1),
    ):
        vector = vector + exchange(vector, axis, size, bit)
    return vector


def shift_depth(tensor, steps):
    return lax.ppermute(tensor, "seq", [(i, (i + 2 * steps) % SEQ) for i in range(SEQ)])


def swap_cores(tensor):
    return exchange(tensor, "seq", SEQ, 1)


def after(tensors, *earlier):
    return lax.optimization_barrier((tensors, earlier))[0]


def per_device(qkv, cotangent, w_proj, clip_levels):
    place = lax.axis_index("seq")
    place_vector = place.astype(jnp.int32).reshape(1)
    clip = clip_levels.reshape(1, D)
    own = cotangent[0]
    own_rows = lax.optimization_barrier(
        lax.dynamic_slice_in_dim(w_proj, place * CHANNELS, CHANNELS, axis=0)
    )
    send = qkv[0].reshape(3, TOKENS, SEQ, LOCAL_HEADS, HEAD_DIM).transpose(2, 3, 0, 1, 4)
    heads = lax.all_to_all(send, "seq", split_axis=0, concat_axis=0, tiled=True)
    weight_max = jnp.max(jnp.abs(own_rows), axis=1).astype(jnp.float32)
    weight_max = weight_max.reshape(LOCAL_HEADS, 1, 128)
    own_swapped = swap_cores(own)
    own_1, weight_max = after((own, weight_max), heads)
    before = shift_depth(own_1, 1)
    behind = shift_depth(own_1, -1)
    weights, out, message = forward(heads, weight_max)
    for bit in (1, 2, 4):
        message = jnp.maximum(message, exchange(message, "dp", DP, bit))
    before, behind = after((before, behind), message)
    halves, message = lax.optimization_barrier(((before[:HALF], behind[HALF:]), message))
    far_low = shift_depth(halves[0], 1)
    far_high = shift_depth(halves[1], -1)
    message = jnp.maximum(message, exchange(message, "dp", DP, 8))
    pieces = [own, before, behind, far_low, far_high, own_swapped]
    pieces += [swap_cores(piece) for piece in (before, behind)]
    moved = [exchange(message, "seq", SEQ, bits) for bits in (2, 4, 6)]
    bound = jnp.maximum(jnp.maximum(message, moved[0]), jnp.maximum(moved[1], moved[2]))
    far_low, far_high, bound = lax.optimization_barrier((far_low, far_high, bound))
    pieces += [swap_cores(piece) for piece in (far_low, far_high)]
    bound = jnp.maximum(bound, exchange(bound, "seq", SEQ, 1))
    grad_out, vector = projection(place_vector, message, bound, clip, out, own_rows, pieces)
    back = backward(heads, weights, out, grad_out)
    back, vector = lax.optimization_barrier((back, total_over_depth(vector)))
    received = lax.all_to_all(back, "seq", split_axis=0, concat_axis=0, tiled=True)
    vector = total_over_rest(vector)[0]
    grad_qkv = received.transpose(2, 3, 0, 1, 4).reshape(1, 3, TOKENS, HEADS, HEAD_DIM)
    return (grad_qkv, vector[: HEADS * HEAD_DIM], vector[HEADS * HEAD_DIM :])


def solution(mesh):
    in_specs = (P("dp", None, "seq", None, None), P("dp", "seq", None), P(), P())
    out_specs = (P("dp", None, "seq", None, None), P(), P())
    return jax.shard_map(
        per_device, mesh=mesh, in_specs=in_specs, out_specs=out_specs, check_vma=False
    )
```

```python
import math

import jax
import jax.numpy as jnp
from jax import lax
from jax.experimental import pallas as pl
from jax.experimental.pallas import tpu as pltpu
from jax.sharding import PartitionSpec as P

HEADS = 16
HEAD_DIM = 128
SEQ = 8
DP = 16
LOCAL_HEADS = 2
CHANNELS = LOCAL_HEADS * HEAD_DIM
TOKENS = 128
LEN = 1024
D = 3072
BLOCK = 256
NUM_BLOCKS = LEN // BLOCK
epsilon = 1e-05
act_fraction = 0.5
SCALE = HEAD_DIM ** (-0.5)
EXP2_SCALE = SCALE * math.log2(math.e)

NN = (((1,), (0,)), ((), ()))
NT = (((1,), (1,)), ((), ()))
TN = (((0,), (0,)), ((), ()))
MIB = 1 << 20
VMEM_LIMIT = 24 * MIB


def dot(lhs, rhs, dims):
    return lax.dot_general(lhs, rhs, dims, preferred_element_type=jnp.float32)


def to_row(column):
    return jnp.broadcast_to(column, (column.shape[0], 128)).T[0:1]


def to_column(row):
    return jnp.broadcast_to(row, (128, row.shape[1])).T[:, 0:1]


def forward_kernel(y_ref, weight_max_ref, p_ref, out_ref, message_ref):
    keys = y_ref[:, 0, 1].reshape(LEN, HEAD_DIM)
    values = y_ref[:, 0, 2].reshape(LEN, HEAD_DIM)
    queries = y_ref[:, 0, 0].reshape(LEN, HEAD_DIM)
    scores = dot(keys, queries, NT)
    row_top = jnp.max(scores, axis=0, keepdims=True)
    exponent = jnp.exp2((scores - row_top) * EXP2_SCALE)
    total = jnp.sum(exponent, axis=0, keepdims=True)
    weights = (exponent * (1.0 / total)).astype(jnp.bfloat16)
    p_ref[0] = weights
    mixed = dot(values, weights, TN).astype(jnp.bfloat16)
    out_ref[0] = mixed
    top = jnp.max(jnp.abs(mixed.astype(jnp.float32)), axis=1, keepdims=True)
    act_row = to_row(top)
    bound = jnp.max(
        jnp.sqrt((act_row + epsilon) * (weight_max_ref[0] + epsilon)), axis=1, keepdims=True
    )
    head = pl.program_id(0)

    @pl.when(head == 0)
    def _():
        message_ref[...] = jnp.zeros_like(message_ref)

    message_ref[pl.ds(head, 1)] = act_row
    message_ref[2:3] = jnp.maximum(message_ref[2:3], bound)


def forward(heads, weight_max):
    return pl.pallas_call(
        forward_kernel,
        grid=(LOCAL_HEADS,),
        in_specs=[
            pl.BlockSpec((SEQ, 1, 3, TOKENS, HEAD_DIM), lambda h: (0, h, 0, 0, 0)),
            pl.BlockSpec((1, 1, 128), lambda h: (h, 0, 0)),
        ],
        out_specs=[
            pl.BlockSpec((1, LEN, LEN), lambda h: (h, 0, 0)),
            pl.BlockSpec((1, HEAD_DIM, LEN), lambda h: (h, 0, 0)),
            pl.BlockSpec((8, 128), lambda h: (0, 0)),
        ],
        out_shape=[
            jax.ShapeDtypeStruct((LOCAL_HEADS, LEN, LEN), jnp.bfloat16),
            jax.ShapeDtypeStruct((LOCAL_HEADS, HEAD_DIM, LEN), jnp.bfloat16),
            jax.ShapeDtypeStruct((8, 128), jnp.float32),
        ],
        compiler_params=pltpu.CompilerParams(vmem_limit_bytes=VMEM_LIMIT),
        cost_estimate=pl.CostEstimate(
            flops=2 * 2 * LOCAL_HEADS * LEN * LEN * HEAD_DIM,
            bytes_accessed=6 * MIB,
            transcendentals=LOCAL_HEADS * LEN * LEN,
        ),
        name="attend_forward",
    )(heads, weight_max)


HALF = TOKENS // 2
WIDTH = 512


def projection_kernel(place_ref, message_ref, bound_ref, clip_ref, out_ref, own_ref, *rest):
    pieces = rest[:10]
    grad_ref, vec_ref, cot_ref, wq_ref, tanh_ref, quant_ref, sem = rest[10:]
    place = place_ref[0]
    depth = place // 2
    core = place % 2
    copies = []
    for k, piece in enumerate(pieces):
        kind, sibling = k % 5, k // 5
        rows = TOKENS if kind < 3 else HALF
        source = (depth + (0, 3, 1, 2, 2)[kind]) % 4
        first = (source * 2 + (core + sibling) % 2) * TOKENS + (HALF if kind == 4 else 0)
        copy = pltpu.make_async_copy(
            piece, cot_ref.at[pl.ds(pl.multiple_of(first, HALF), rows)], sem.at[k]
        )
        copy.start()
        copies.append(copy)
    act_clip = act_fraction * bound_ref[2:3, 0:1]
    act_column = jnp.concatenate(
        [to_column(message_ref[0:1]), to_column(message_ref[1:2])], axis=0
    )
    weight_max = None
    for j in range(D // WIDTH):
        weight = own_ref[:, j * WIDTH : (j + 1) * WIDTH]
        top = jnp.max(jnp.abs(weight.astype(jnp.float32)), axis=1, keepdims=True)
        weight_max = top if weight_max is None else jnp.maximum(weight_max, top)
    smooth = jnp.sqrt((act_column + epsilon) / (weight_max + epsilon))
    for j in range(D // WIDTH):
        columns = slice(j * WIDTH, (j + 1) * WIDTH)
        clip = clip_ref[:, columns]
        weight = own_ref[:, columns].astype(jnp.float32)
        tanh = jnp.tanh((smooth * weight) * (1.0 / clip))
        tanh_ref[:, columns] = tanh
        wq_ref[:, columns] = (clip * tanh).astype(jnp.bfloat16)
    inverse = 1.0 / smooth
    inner = inverse / act_clip
    for copy in copies:
        copy.wait()
    act_part = None
    for t in range(NUM_BLOCKS):
        tokens = slice(t * BLOCK, (t + 1) * BLOCK)
        grad_act = dot(wq_ref[...], cot_ref[tokens], NT)
        out = out_ref[:, :, tokens].reshape(CHANNELS, BLOCK).astype(jnp.float32)
        tanh = jnp.tanh(out * inner)
        quant_ref[:, tokens] = (act_clip * tanh).astype(jnp.bfloat16)
        smoothed = grad_act * (1.0 - tanh * tanh)
        part = jnp.sum(smoothed * out, axis=1, keepdims=True)
        act_part = part if act_part is None else act_part + part
        grad_ref[:, :, tokens] = (
            (smoothed * inverse).astype(jnp.bfloat16).reshape(LOCAL_HEADS, HEAD_DIM, BLOCK)
        )
    smooth_part = -act_part * (inverse * inverse)
    vec_ref[...] = jnp.zeros_like(vec_ref)
    for j in range(D // WIDTH):
        columns = slice(j * WIDTH, (j + 1) * WIDTH)
        weight = own_ref[:, columns].astype(jnp.float32)
        grad_weight = dot(quant_ref[...], cot_ref[:, columns], NN)
        ratio = (smooth * weight) * (1.0 / clip_ref[:, columns])
        tanh = tanh_ref[:, columns]
        slope = 1.0 - tanh * tanh
        vec_ref[:, HEADS * HEAD_DIM + j * WIDTH : HEADS * HEAD_DIM + (j + 1) * WIDTH] = jnp.sum(
            grad_weight * (tanh - ratio * slope), axis=0, keepdims=True
        )
        smooth_part += jnp.sum(grad_weight * slope * weight, axis=1, keepdims=True)
    vec_ref[:, pl.ds(pl.multiple_of(place * CHANNELS, CHANNELS), CHANNELS)] = to_row(smooth_part)


def projection(place, message, bound, clip, out, own_rows, pieces):
    vmem = pl.BlockSpec(memory_space=pltpu.VMEM)
    hbm = pl.BlockSpec(memory_space=pl.ANY)
    return pl.pallas_call(
        projection_kernel,
        in_specs=[pl.BlockSpec(memory_space=pltpu.SMEM), vmem, vmem, vmem, vmem, vmem] + [hbm] * 10,
        out_specs=[vmem, vmem],
        out_shape=[
            jax.ShapeDtypeStruct((LOCAL_HEADS, HEAD_DIM, LEN), jnp.bfloat16),
            jax.ShapeDtypeStruct((1, HEADS * HEAD_DIM + D), jnp.float32),
        ],
        scratch_shapes=[
            pltpu.VMEM((LEN, D), jnp.bfloat16),
            pltpu.VMEM((CHANNELS, D), jnp.bfloat16),
            pltpu.VMEM((CHANNELS, D), jnp.float32),
            pltpu.VMEM((CHANNELS, LEN), jnp.bfloat16),
            pltpu.SemaphoreType.DMA((10,)),
        ],
        compiler_params=pltpu.CompilerParams(vmem_limit_bytes=VMEM_LIMIT),
        cost_estimate=pl.CostEstimate(
            flops=2 * 2 * CHANNELS * LEN * D,
            bytes_accessed=9 * MIB,
            transcendentals=CHANNELS * (D + LEN),
        ),
        name="projection_backward",
    )(place, message, bound, clip, out, own_rows, *pieces)


def backward_kernel(y_ref, p_ref, out_ref, grad_ref, z_ref, ds_ref):
    keys = y_ref[:, 0, 1].reshape(LEN, HEAD_DIM)
    values = y_ref[:, 0, 2].reshape(LEN, HEAD_DIM)
    for b in range(LEN // WIDTH):
        columns = pl.ds(b * WIDTH, WIDTH)
        grad_out = grad_ref[0, :, columns]
        delta = jnp.sum(
            grad_out.astype(jnp.float32) * out_ref[0, :, columns].astype(jnp.float32),
            axis=0,
            keepdims=True,
        )
        grad_weights = dot(values, grad_out, NN)
        weights = p_ref[0, :, columns].astype(jnp.float32)
        ds_ref[:, columns] = (weights * (grad_weights - delta)).astype(jnp.bfloat16)
    queries = y_ref[:, 0, 0].reshape(LEN, HEAD_DIM)
    grad_query = (dot(keys, ds_ref[...], TN) * SCALE).astype(jnp.bfloat16)
    z_ref[:, 0, 0] = grad_query.T.reshape(SEQ, TOKENS, HEAD_DIM)
    grad_value = dot(p_ref[0], grad_ref[0], NT)
    z_ref[:, 0, 2] = grad_value.astype(jnp.bfloat16).reshape(SEQ, TOKENS, HEAD_DIM)
    grad_key = dot(ds_ref[...], queries, NN) * SCALE
    z_ref[:, 0, 1] = grad_key.astype(jnp.bfloat16).reshape(SEQ, TOKENS, HEAD_DIM)


def backward(heads, weights, out, grad_out):
    return pl.pallas_call(
        backward_kernel,
        grid=(LOCAL_HEADS,),
        in_specs=[
            pl.BlockSpec((SEQ, 1, 3, TOKENS, HEAD_DIM), lambda h: (0, h, 0, 0, 0)),
            pl.BlockSpec((1, LEN, LEN), lambda h: (h, 0, 0)),
            pl.BlockSpec((1, HEAD_DIM, LEN), lambda h: (h, 0, 0)),
            pl.BlockSpec((1, HEAD_DIM, LEN), lambda h: (h, 0, 0)),
        ],
        out_specs=pl.BlockSpec((SEQ, 1, 3, TOKENS, HEAD_DIM), lambda h: (0, h, 0, 0, 0)),
        out_shape=jax.ShapeDtypeStruct(
            (SEQ, LOCAL_HEADS, 3, TOKENS, HEAD_DIM), jnp.bfloat16
        ),
        scratch_shapes=[pltpu.VMEM((LEN, LEN), jnp.bfloat16)],
        compiler_params=pltpu.CompilerParams(vmem_limit_bytes=VMEM_LIMIT),
        cost_estimate=pl.CostEstimate(
            flops=4 * 2 * LOCAL_HEADS * LEN * LEN * HEAD_DIM,
            bytes_accessed=8 * MIB,
            transcendentals=0,
        ),
        name="attend_backward",
    )(heads, weights, out, grad_out)


def exchange(tensor, axis, size, bits):
    return lax.ppermute(tensor, axis, [(i, i ^ bits) for i in range(size)])


def total_over_depth(vector):
    moved = [exchange(vector, "seq", SEQ, bits) for bits in (2, 4, 6)]
    return (vector + moved[0]) + (moved[1] + moved[2])


def total_over_rest(vector):
    for axis, size, bit in (
        ("dp", DP, 1),
        ("dp", DP, 2),
        ("dp", DP, 4),
        ("dp", DP, 8),
        ("seq", SEQ, 1),
    ):
        vector = vector + exchange(vector, axis, size, bit)
    return vector


def shift_depth(tensor, steps):
    return lax.ppermute(tensor, "seq", [(i, (i + 2 * steps) % SEQ) for i in range(SEQ)])


def swap_cores(tensor):
    return exchange(tensor, "seq", SEQ, 1)


def after(tensors, *earlier):
    return lax.optimization_barrier((tensors, earlier))[0]


def per_device(qkv, cotangent, w_proj, clip_levels):
    place = lax.axis_index("seq")
    place_vector = place.astype(jnp.int32).reshape(1)
    clip = clip_levels.reshape(1, D)
    own = cotangent[0]
    own_rows = lax.optimization_barrier(
        lax.dynamic_slice_in_dim(w_proj, place * CHANNELS, CHANNELS, axis=0)
    )
    send = qkv[0].reshape(3, TOKENS, SEQ, LOCAL_HEADS, HEAD_DIM).transpose(2, 3, 0, 1, 4)
    heads = lax.all_to_all(send, "seq", split_axis=0, concat_axis=0, tiled=True)
    weight_max = jnp.max(jnp.abs(own_rows), axis=1).astype(jnp.float32)
    weight_max = weight_max.reshape(LOCAL_HEADS, 1, 128)
    own_swapped = swap_cores(own)
    own_1, weight_max = after((own, weight_max), heads)
    before = shift_depth(own_1, 1)
    behind = shift_depth(own_1, -1)
    weights, out, message = forward(heads, weight_max)
    is_bound = lax.broadcasted_iota(jnp.int32, message.shape, 0) == 2
    for bit in (1, 2, 4):
        message = jnp.maximum(message, exchange(message, "dp", DP, bit))
    before, behind = after((before, behind), message)
    halves, message = lax.optimization_barrier(((before[:HALF], behind[HALF:]), message))
    far_low = shift_depth(halves[0], 1)
    far_high = shift_depth(halves[1], -1)
    moved = [exchange(message, "seq", SEQ, bits) for bits in (2, 4, 6)]
    bound = jnp.maximum(jnp.maximum(message, moved[0]), jnp.maximum(moved[1], moved[2]))
    message = jnp.where(is_bound, bound, message)
    for bit in (8,):
        message = jnp.maximum(message, exchange(message, "dp", DP, bit))
    far_low, far_high, message = lax.optimization_barrier((far_low, far_high, message))
    pair = jnp.maximum(message, exchange(message, "seq", SEQ, 1))
    message = jnp.where(is_bound, pair, message)
    pieces = [own, before, behind, far_low, far_high, own_swapped]
    pieces += [swap_cores(piece) for piece in (before, behind, far_low, far_high)]
    grad_out, vector = projection(place_vector, message, message, clip, out, own_rows, pieces)
    back = backward(heads, weights, out, grad_out)
    back, vector = lax.optimization_barrier((back, total_over_depth(vector)))
    received = lax.all_to_all(back, "seq", split_axis=0, concat_axis=0, tiled=True)
    vector = total_over_rest(vector)[0]
    grad_qkv = received.transpose(2, 3, 0, 1, 4).reshape(1, 3, TOKENS, HEADS, HEAD_DIM)
    return (grad_qkv, vector[: HEADS * HEAD_DIM], vector[HEADS * HEAD_DIM :])


def solution(mesh):
    in_specs = (P("dp", None, "seq", None, None), P("dp", "seq", None), P(), P())
    out_specs = (P("dp", None, "seq", None, None), P(), P())
    return jax.shard_map(
        per_device, mesh=mesh, in_specs=in_specs, out_specs=out_specs, check_vma=False
    )
```

```python
import math

import jax
import jax.numpy as jnp
from jax import lax
from jax.experimental import pallas as pl
from jax.experimental.pallas import tpu as pltpu
from jax.sharding import PartitionSpec as P

HEADS = 16
HEAD_DIM = 128
SEQ = 8
DP = 16
LOCAL_HEADS = 2
CHANNELS = LOCAL_HEADS * HEAD_DIM
TOKENS = 128
LEN = 1024
D = 3072
BLOCK = 256
NUM_BLOCKS = LEN // BLOCK
epsilon = 1e-05
act_fraction = 0.5
SCALE = HEAD_DIM ** (-0.5)
EXP2_SCALE = SCALE * math.log2(math.e)

NN = (((1,), (0,)), ((), ()))
NT = (((1,), (1,)), ((), ()))
TN = (((0,), (0,)), ((), ()))
MIB = 1 << 20
VMEM_LIMIT = 24 * MIB


def dot(lhs, rhs, dims):
    return lax.dot_general(lhs, rhs, dims, preferred_element_type=jnp.float32)


def to_row(column):
    return jnp.broadcast_to(column, (column.shape[0], 128)).T[0:1]


def to_column(row):
    return jnp.broadcast_to(row, (128, row.shape[1])).T[:, 0:1]


def forward_kernel(y_ref, weight_max_ref, p_ref, out_ref, message_ref):
    scores = []
    for head in range(LOCAL_HEADS):
        queries = y_ref[:, head, 0].reshape(LEN, HEAD_DIM)
        keys = y_ref[:, head, 1].reshape(LEN, HEAD_DIM)
        scores.append(dot(keys, queries, NT))
    message_ref[...] = jnp.zeros_like(message_ref)
    for head in range(LOCAL_HEADS):
        row_top = jnp.max(scores[head], axis=0, keepdims=True)
        exponent = jnp.exp2((scores[head] - row_top) * EXP2_SCALE)
        total = jnp.sum(exponent, axis=0, keepdims=True)
        weights = (exponent * (1.0 / total)).astype(jnp.bfloat16)
        p_ref[head] = weights
        values = y_ref[:, head, 2].reshape(LEN, HEAD_DIM)
        mixed = dot(values, weights, TN).astype(jnp.bfloat16)
        out_ref[head] = mixed
        act_row = to_row(jnp.max(jnp.abs(mixed.astype(jnp.float32)), axis=1, keepdims=True))
        bound = jnp.max(
            jnp.sqrt((act_row + epsilon) * (weight_max_ref[head] + epsilon)),
            axis=1,
            keepdims=True,
        )
        message_ref[head : head + 1] = act_row
        message_ref[2:3] = jnp.maximum(message_ref[2:3], bound)


def forward(heads, weight_max):
    vmem = pl.BlockSpec(memory_space=pltpu.VMEM)
    return pl.pallas_call(
        forward_kernel,
        in_specs=[vmem] * 2,
        out_specs=[vmem] * 3,
        out_shape=[
            jax.ShapeDtypeStruct((LOCAL_HEADS, LEN, LEN), jnp.bfloat16),
            jax.ShapeDtypeStruct((LOCAL_HEADS, HEAD_DIM, LEN), jnp.bfloat16),
            jax.ShapeDtypeStruct((8, 128), jnp.float32),
        ],
        compiler_params=pltpu.CompilerParams(vmem_limit_bytes=28 * MIB),
        cost_estimate=pl.CostEstimate(
            flops=2 * 2 * LOCAL_HEADS * LEN * LEN * HEAD_DIM,
            bytes_accessed=6 * MIB,
            transcendentals=LOCAL_HEADS * LEN * LEN,
        ),
        name="attend_forward",
    )(heads, weight_max)


HALF = TOKENS // 2
WIDTH = 512


def projection_kernel(place_ref, message_ref, bound_ref, clip_ref, out_ref, own_ref, *rest):
    pieces = rest[:10]
    grad_ref, vec_ref, cot_ref, wq_ref, tanh_ref, quant_ref = rest[10:]
    place = place_ref[0]
    depth = place // 2
    core = place % 2
    for k, piece in enumerate(pieces):
        kind, sibling = k % 5, k // 5
        rows = TOKENS if kind < 3 else HALF
        source = (depth + (0, 3, 1, 2, 2)[kind]) % 4
        first = (source * 2 + (core + sibling) % 2) * TOKENS + (HALF if kind == 4 else 0)
        cot_ref[pl.ds(pl.multiple_of(first, HALF), rows)] = piece[...]
    act_clip = act_fraction * bound_ref[2:3, 0:1]
    act_column = jnp.concatenate(
        [to_column(message_ref[0:1]), to_column(message_ref[1:2])], axis=0
    )
    weight_max = None
    for j in range(D // WIDTH):
        weight = own_ref[:, j * WIDTH : (j + 1) * WIDTH]
        top = jnp.max(jnp.abs(weight.astype(jnp.float32)), axis=1, keepdims=True)
        weight_max = top if weight_max is None else jnp.maximum(weight_max, top)
    smooth = jnp.sqrt((act_column + epsilon) / (weight_max + epsilon))
    for j in range(D // WIDTH):
        columns = slice(j * WIDTH, (j + 1) * WIDTH)
        clip = clip_ref[:, columns]
        weight = own_ref[:, columns].astype(jnp.float32)
        tanh = jnp.tanh((smooth * weight) * (1.0 / clip))
        tanh_ref[:, columns] = tanh
        wq_ref[:, columns] = (clip * tanh).astype(jnp.bfloat16)
    inverse = 1.0 / smooth
    inner = inverse / act_clip
    act_part = None
    for t in range(NUM_BLOCKS):
        tokens = slice(t * BLOCK, (t + 1) * BLOCK)
        grad_act = dot(wq_ref[...], cot_ref[tokens], NT)
        out = out_ref[:, :, tokens].reshape(CHANNELS, BLOCK).astype(jnp.float32)
        tanh = jnp.tanh(out * inner)
        quant_ref[:, tokens] = (act_clip * tanh).astype(jnp.bfloat16)
        smoothed = grad_act * (1.0 - tanh * tanh)
        part = jnp.sum(smoothed * out, axis=1, keepdims=True)
        act_part = part if act_part is None else act_part + part
        grad_ref[:, :, tokens] = (
            (smoothed * inverse).astype(jnp.bfloat16).reshape(LOCAL_HEADS, HEAD_DIM, BLOCK)
        )
    smooth_part = -act_part * (inverse * inverse)
    vec_ref[...] = jnp.zeros_like(vec_ref)
    for j in range(D // WIDTH):
        columns = slice(j * WIDTH, (j + 1) * WIDTH)
        weight = own_ref[:, columns].astype(jnp.float32)
        grad_weight = dot(quant_ref[...], cot_ref[:, columns], NN)
        ratio = (smooth * weight) * (1.0 / clip_ref[:, columns])
        tanh = tanh_ref[:, columns]
        slope = 1.0 - tanh * tanh
        vec_ref[:, HEADS * HEAD_DIM + j * WIDTH : HEADS * HEAD_DIM + (j + 1) * WIDTH] = jnp.sum(
            grad_weight * (tanh - ratio * slope), axis=0, keepdims=True
        )
        smooth_part += jnp.sum(grad_weight * slope * weight, axis=1, keepdims=True)
    vec_ref[:, pl.ds(pl.multiple_of(place * CHANNELS, CHANNELS), CHANNELS)] = to_row(smooth_part)


def projection(place, message, bound, clip, out, own_rows, pieces):
    vmem = pl.BlockSpec(memory_space=pltpu.VMEM)
    return pl.pallas_call(
        projection_kernel,
        in_specs=[pl.BlockSpec(memory_space=pltpu.SMEM), vmem, vmem, vmem, vmem, vmem]+ [vmem] * 10,
        out_specs=[vmem, vmem],
        out_shape=[
            jax.ShapeDtypeStruct((LOCAL_HEADS, HEAD_DIM, LEN), jnp.bfloat16),
            jax.ShapeDtypeStruct((1, HEADS * HEAD_DIM + D), jnp.float32),
        ],
        scratch_shapes=[
            pltpu.VMEM((LEN, D), jnp.bfloat16),
            pltpu.VMEM((CHANNELS, D), jnp.bfloat16),
            pltpu.VMEM((CHANNELS, D), jnp.float32),
            pltpu.VMEM((CHANNELS, LEN), jnp.bfloat16),
        ],
        compiler_params=pltpu.CompilerParams(vmem_limit_bytes=VMEM_LIMIT),
        cost_estimate=pl.CostEstimate(
            flops=2 * 2 * CHANNELS * LEN * D,
            bytes_accessed=9 * MIB,
            transcendentals=CHANNELS * (D + LEN),
        ),
        name="projection_backward",
    )(place, message, bound, clip, out, own_rows, *pieces)


def backward_kernel(y_ref, p_ref, out_ref, grad_ref, result_ref, z_ref, ds_ref, sem):
    copies = []

    def send(head, which):
        copy = pltpu.make_async_copy(
            z_ref.at[:, head, which], result_ref.at[:, head, which], sem.at[head, which]
        )
        copy.start()
        copies.append(copy)

    for head in range(LOCAL_HEADS):
        values = y_ref[:, head, 2].reshape(LEN, HEAD_DIM)
        grad_value = dot(p_ref[head], grad_ref[head], NT)
        z_ref[:, head, 2] = grad_value.astype(jnp.bfloat16).reshape(SEQ, TOKENS, HEAD_DIM)
        send(head, 2)
        for b in range(LEN // WIDTH):
            columns = pl.ds(b * WIDTH, WIDTH)
            grad_out = grad_ref[head, :, columns]
            delta = jnp.sum(
                grad_out.astype(jnp.float32) * out_ref[head, :, columns].astype(jnp.float32),
                axis=0,
                keepdims=True,
            )
            grad_weights = dot(values, grad_out, NN)
            weights = p_ref[head, :, columns].astype(jnp.float32)
            ds_ref[head, :, columns] = (weights * (grad_weights - delta)).astype(jnp.bfloat16)
    for head in range(LOCAL_HEADS):
        queries = y_ref[:, head, 0].reshape(LEN, HEAD_DIM)
        keys = y_ref[:, head, 1].reshape(LEN, HEAD_DIM)
        grad_query = (dot(keys, ds_ref[head], TN) * SCALE).astype(jnp.bfloat16)
        z_ref[:, head, 0] = grad_query.T.reshape(SEQ, TOKENS, HEAD_DIM)
        send(head, 0)
        grad_key = dot(ds_ref[head], queries, NN) * SCALE
        z_ref[:, head, 1] = grad_key.astype(jnp.bfloat16).reshape(SEQ, TOKENS, HEAD_DIM)
        send(head, 1)
    for copy in copies:
        copy.wait()


def backward(heads, weights, out, grad_out):
    vmem = pl.BlockSpec(memory_space=pltpu.VMEM)
    return pl.pallas_call(
        backward_kernel,
        in_specs=[vmem] * 4,
        out_specs=pl.BlockSpec(memory_space=pl.ANY),
        out_shape=jax.ShapeDtypeStruct(
            (SEQ, LOCAL_HEADS, 3, TOKENS, HEAD_DIM), jnp.bfloat16
        ),
        scratch_shapes=[
            pltpu.VMEM((SEQ, LOCAL_HEADS, 3, TOKENS, HEAD_DIM), jnp.bfloat16),
            pltpu.VMEM((LOCAL_HEADS, LEN, LEN), jnp.bfloat16),
            pltpu.SemaphoreType.DMA((LOCAL_HEADS, 3)),
        ],
        compiler_params=pltpu.CompilerParams(vmem_limit_bytes=28 * MIB),
        cost_estimate=pl.CostEstimate(
            flops=4 * 2 * LOCAL_HEADS * LEN * LEN * HEAD_DIM,
            bytes_accessed=8 * MIB,
            transcendentals=0,
        ),
        name="attend_backward",
    )(heads, weights, out, grad_out)


def exchange(tensor, axis, size, bits):
    return lax.ppermute(tensor, axis, [(i, i ^ bits) for i in range(size)])


def total_over_depth(vector):
    moved = [exchange(vector, "seq", SEQ, bits) for bits in (2, 4, 6)]
    return (vector + moved[0]) + (moved[1] + moved[2])


def total_over_rest(vector):
    for axis, size, bit in (
        ("dp", DP, 1),
        ("dp", DP, 2),
        ("dp", DP, 4),
        ("dp", DP, 8),
        ("seq", SEQ, 1),
    ):
        vector = vector + exchange(vector, axis, size, bit)
    return vector


def shift_depth(tensor, steps):
    return lax.ppermute(tensor, "seq", [(i, (i + 2 * steps) % SEQ) for i in range(SEQ)])


def swap_cores(tensor):
    return exchange(tensor, "seq", SEQ, 1)


def after(tensors, *earlier):
    return lax.optimization_barrier((tensors, earlier))[0]


def per_device(qkv, cotangent, w_proj, clip_levels):
    place = lax.axis_index("seq")
    place_vector = place.astype(jnp.int32).reshape(1)
    clip = clip_levels.reshape(1, D)
    own = cotangent[0]
    own_rows = lax.optimization_barrier(
        lax.dynamic_slice_in_dim(w_proj, place * CHANNELS, CHANNELS, axis=0)
    )
    send = qkv[0].reshape(3, TOKENS, SEQ, LOCAL_HEADS, HEAD_DIM).transpose(2, 3, 0, 1, 4)
    heads = lax.all_to_all(send, "seq", split_axis=0, concat_axis=0, tiled=True)
    weight_max = jnp.max(jnp.abs(own_rows), axis=1).astype(jnp.float32)
    weight_max = weight_max.reshape(LOCAL_HEADS, 1, 128)
    own_swapped = swap_cores(own)
    own_1, weight_max = after((own, weight_max), heads)
    before = shift_depth(own_1, 1)
    behind = shift_depth(own_1, -1)
    weights, out, message = forward(heads, weight_max)
    is_bound = lax.broadcasted_iota(jnp.int32, message.shape, 0) == 2
    for bit in (1, 2, 4):
        message = jnp.maximum(message, exchange(message, "dp", DP, bit))
    before, behind = after((before, behind), message)
    halves, message = lax.optimization_barrier(((before[:HALF], behind[HALF:]), message))
    far_low = shift_depth(halves[0], 1)
    far_high = shift_depth(halves[1], -1)
    moved = [exchange(message, "seq", SEQ, bits) for bits in (2, 4, 6)]
    bound = jnp.maximum(jnp.maximum(message, moved[0]), jnp.maximum(moved[1], moved[2]))
    message = jnp.where(is_bound, bound, message)
    for bit in (8,):
        message = jnp.maximum(message, exchange(message, "dp", DP, bit))
    far_low, far_high, message = lax.optimization_barrier((far_low, far_high, message))
    pair = jnp.maximum(message, exchange(message, "seq", SEQ, 1))
    message = jnp.where(is_bound, pair, message)
    pieces = [own, before, behind, far_low, far_high, own_swapped]
    pieces += [swap_cores(piece) for piece in (before, behind, far_low, far_high)]
    grad_out, vector = projection(place_vector, message, message, clip, out, own_rows, pieces)
    back = backward(heads, weights, out, grad_out)
    back, vector = lax.optimization_barrier((back, total_over_depth(vector)))
    received = lax.all_to_all(back, "seq", split_axis=0, concat_axis=0, tiled=True)
    vector = total_over_rest(vector)[0]
    grad_qkv = received.transpose(2, 3, 0, 1, 4).reshape(1, 3, TOKENS, HEADS, HEAD_DIM)
    return (grad_qkv, vector[: HEADS * HEAD_DIM], vector[HEADS * HEAD_DIM :])


def solution(mesh):
    in_specs = (P("dp", None, "seq", None, None), P("dp", "seq", None), P(), P())
    out_specs = (P("dp", None, "seq", None, None), P(), P())
    return jax.shard_map(
        per_device, mesh=mesh, in_specs=in_specs, out_specs=out_specs, check_vma=False
    )
```

```python
import math

import jax
import jax.numpy as jnp
from jax import lax
from jax.experimental import pallas as pl
from jax.experimental.pallas import tpu as pltpu
from jax.sharding import PartitionSpec as P

HEADS = 16
HEAD_DIM = 128
SEQ = 8
DP = 16
LOCAL_HEADS = 2
CHANNELS = LOCAL_HEADS * HEAD_DIM
TOKENS = 128
LEN = 1024
D = 3072
BLOCK = 256
NUM_BLOCKS = LEN // BLOCK
epsilon = 1e-05
act_fraction = 0.5
SCALE = HEAD_DIM ** (-0.5)
EXP2_SCALE = SCALE * math.log2(math.e)

NN = (((1,), (0,)), ((), ()))
NT = (((1,), (1,)), ((), ()))
TN = (((0,), (0,)), ((), ()))
MIB = 1 << 20
VMEM_LIMIT = 24 * MIB


def dot(lhs, rhs, dims):
    return lax.dot_general(lhs, rhs, dims, preferred_element_type=jnp.float32)


def to_row(column):
    return jnp.broadcast_to(column, (column.shape[0], 128)).T[0:1]


def to_column(row):
    return jnp.broadcast_to(row, (128, row.shape[1])).T[:, 0:1]


def forward_kernel(y_ref, weight_max_ref, p_ref, out_ref, message_ref):
    scores = []
    for head in range(LOCAL_HEADS):
        queries = y_ref[:, head, 0].reshape(LEN, HEAD_DIM)
        keys = y_ref[:, head, 1].reshape(LEN, HEAD_DIM)
        scores.append(dot(keys, queries, NT))
    message_ref[...] = jnp.zeros_like(message_ref)
    for head in range(LOCAL_HEADS):
        row_top = jnp.max(scores[head], axis=0, keepdims=True)
        exponent = jnp.exp2((scores[head] - row_top) * EXP2_SCALE)
        total = jnp.sum(exponent, axis=0, keepdims=True)
        weights = (exponent * (1.0 / total)).astype(jnp.bfloat16)
        p_ref[head] = weights
        values = y_ref[:, head, 2].reshape(LEN, HEAD_DIM)
        mixed = dot(values, weights, TN).astype(jnp.bfloat16)
        out_ref[head] = mixed
        act_row = to_row(jnp.max(jnp.abs(mixed.astype(jnp.float32)), axis=1, keepdims=True))
        bound = jnp.max(
            jnp.sqrt((act_row + epsilon) * (weight_max_ref[head] + epsilon)),
            axis=1,
            keepdims=True,
        )
        message_ref[head : head + 1] = act_row
        message_ref[2:3] = jnp.maximum(message_ref[2:3], bound)


def forward(heads, weight_max):
    vmem = pl.BlockSpec(memory_space=pltpu.VMEM)
    return pl.pallas_call(
        forward_kernel,
        in_specs=[vmem] * 2,
        out_specs=[vmem] * 3,
        out_shape=[
            jax.ShapeDtypeStruct((LOCAL_HEADS, LEN, LEN), jnp.bfloat16),
            jax.ShapeDtypeStruct((LOCAL_HEADS, HEAD_DIM, LEN), jnp.bfloat16),
            jax.ShapeDtypeStruct((8, 128), jnp.float32),
        ],
        compiler_params=pltpu.CompilerParams(vmem_limit_bytes=28 * MIB),
        cost_estimate=pl.CostEstimate(
            flops=2 * 2 * LOCAL_HEADS * LEN * LEN * HEAD_DIM,
            bytes_accessed=6 * MIB,
            transcendentals=LOCAL_HEADS * LEN * LEN,
        ),
        name="attend_forward",
    )(heads, weight_max)


HALF = TOKENS // 2
WIDTH = 512


def projection_kernel(place_ref, message_ref, bound_ref, weight_max_ref, clip_ref, out_ref, own_ref, *rest):
    pieces = rest[:10]
    grad_ref, vec_ref, cot_ref, wq_ref, tanh_ref, quant_ref = rest[10:]
    place = place_ref[0]
    depth = place // 2
    core = place % 2
    for k, piece in enumerate(pieces):
        kind, sibling = k % 5, k // 5
        rows = TOKENS if kind < 3 else HALF
        source = (depth + (0, 3, 1, 2, 2)[kind]) % 4
        first = (source * 2 + (core + sibling) % 2) * TOKENS + (HALF if kind == 4 else 0)
        cot_ref[pl.ds(pl.multiple_of(first, HALF), rows)] = piece[...]
    act_clip = act_fraction * bound_ref[2:3, 0:1]
    act_column = jnp.concatenate(
        [to_column(message_ref[0:1]), to_column(message_ref[1:2])], axis=0
    )
    weight_max = jnp.concatenate(
        [to_column(weight_max_ref[0]), to_column(weight_max_ref[1])], axis=0
    )
    smooth = jnp.sqrt((act_column + epsilon) / (weight_max + epsilon))
    for j in range(D // WIDTH):
        columns = slice(j * WIDTH, (j + 1) * WIDTH)
        clip = clip_ref[:, columns]
        weight = own_ref[:, columns].astype(jnp.float32)
        tanh = jnp.tanh((smooth * weight) * (1.0 / clip))
        tanh_ref[:, columns] = tanh
        wq_ref[:, columns] = (clip * tanh).astype(jnp.bfloat16)
    inverse = 1.0 / smooth
    inner = inverse / act_clip
    act_part = None
    for t in range(NUM_BLOCKS):
        tokens = slice(t * BLOCK, (t + 1) * BLOCK)
        grad_act = dot(wq_ref[...], cot_ref[tokens], NT)
        out = out_ref[:, :, tokens].reshape(CHANNELS, BLOCK).astype(jnp.float32)
        tanh = jnp.tanh(out * inner)
        quant_ref[:, tokens] = (act_clip * tanh).astype(jnp.bfloat16)
        smoothed = grad_act * (1.0 - tanh * tanh)
        part = jnp.sum(smoothed * out, axis=1, keepdims=True)
        act_part = part if act_part is None else act_part + part
        grad_ref[:, :, tokens] = (
            (smoothed * inverse).astype(jnp.bfloat16).reshape(LOCAL_HEADS, HEAD_DIM, BLOCK)
        )
    smooth_part = -act_part * (inverse * inverse)
    vec_ref[...] = jnp.zeros_like(vec_ref)
    for j in range(D // WIDTH):
        columns = slice(j * WIDTH, (j + 1) * WIDTH)
        weight = own_ref[:, columns].astype(jnp.float32)
        grad_weight = dot(quant_ref[...], cot_ref[:, columns], NN)
        ratio = (smooth * weight) * (1.0 / clip_ref[:, columns])
        tanh = tanh_ref[:, columns]
        slope = 1.0 - tanh * tanh
        vec_ref[:, HEADS * HEAD_DIM + j * WIDTH : HEADS * HEAD_DIM + (j + 1) * WIDTH] = jnp.sum(
            grad_weight * (tanh - ratio * slope), axis=0, keepdims=True
        )
        smooth_part += jnp.sum(grad_weight * slope * weight, axis=1, keepdims=True)
    vec_ref[:, pl.ds(pl.multiple_of(place * CHANNELS, CHANNELS), CHANNELS)] = to_row(smooth_part)


def projection(place, message, bound, weight_max, clip, out, own_rows, pieces):
    vmem = pl.BlockSpec(memory_space=pltpu.VMEM)
    return pl.pallas_call(
        projection_kernel,
        in_specs=[pl.BlockSpec(memory_space=pltpu.SMEM), vmem, vmem, vmem, vmem, vmem, vmem]+ [vmem] * 10,
        out_specs=[vmem, vmem],
        out_shape=[
            jax.ShapeDtypeStruct((LOCAL_HEADS, HEAD_DIM, LEN), jnp.bfloat16),
            jax.ShapeDtypeStruct((1, HEADS * HEAD_DIM + D), jnp.float32),
        ],
        scratch_shapes=[
            pltpu.VMEM((LEN, D), jnp.bfloat16),
            pltpu.VMEM((CHANNELS, D), jnp.bfloat16),
            pltpu.VMEM((CHANNELS, D), jnp.float32),
            pltpu.VMEM((CHANNELS, LEN), jnp.bfloat16),
        ],
        compiler_params=pltpu.CompilerParams(vmem_limit_bytes=VMEM_LIMIT),
        cost_estimate=pl.CostEstimate(
            flops=2 * 2 * CHANNELS * LEN * D,
            bytes_accessed=9 * MIB,
            transcendentals=CHANNELS * (D + LEN),
        ),
        name="projection_backward",
    )(place, message, bound, weight_max, clip, out, own_rows, *pieces)


def backward_kernel(y_ref, p_ref, out_ref, grad_ref, result_ref, z_ref, ds_ref, sem):
    copies = []

    def send(head, which):
        copy = pltpu.make_async_copy(
            z_ref.at[:, head, which], result_ref.at[:, head, which], sem.at[head, which]
        )
        copy.start()
        copies.append(copy)

    for head in range(LOCAL_HEADS):
        values = y_ref[:, head, 2].reshape(LEN, HEAD_DIM)
        grad_value = dot(p_ref[head], grad_ref[head], NT)
        z_ref[:, head, 2] = grad_value.astype(jnp.bfloat16).reshape(SEQ, TOKENS, HEAD_DIM)
        send(head, 2)
        for b in range(LEN // WIDTH):
            columns = pl.ds(b * WIDTH, WIDTH)
            grad_out = grad_ref[head, :, columns]
            delta = jnp.sum(
                grad_out.astype(jnp.float32) * out_ref[head, :, columns].astype(jnp.float32),
                axis=0,
                keepdims=True,
            )
            grad_weights = dot(values, grad_out, NN)
            weights = p_ref[head, :, columns].astype(jnp.float32)
            ds_ref[head, :, columns] = (weights * (grad_weights - delta)).astype(jnp.bfloat16)
    for head in range(LOCAL_HEADS):
        queries = y_ref[:, head, 0].reshape(LEN, HEAD_DIM)
        keys = y_ref[:, head, 1].reshape(LEN, HEAD_DIM)
        grad_query = (dot(keys, ds_ref[head], TN) * SCALE).astype(jnp.bfloat16)
        z_ref[:, head, 0] = grad_query.T.reshape(SEQ, TOKENS, HEAD_DIM)
        send(head, 0)
        grad_key = dot(ds_ref[head], queries, NN) * SCALE
        z_ref[:, head, 1] = grad_key.astype(jnp.bfloat16).reshape(SEQ, TOKENS, HEAD_DIM)
        send(head, 1)
    for copy in copies:
        copy.wait()


def backward(heads, weights, out, grad_out):
    vmem = pl.BlockSpec(memory_space=pltpu.VMEM)
    return pl.pallas_call(
        backward_kernel,
        in_specs=[vmem] * 4,
        out_specs=pl.BlockSpec(memory_space=pl.ANY),
        out_shape=jax.ShapeDtypeStruct(
            (SEQ, LOCAL_HEADS, 3, TOKENS, HEAD_DIM), jnp.bfloat16
        ),
        scratch_shapes=[
            pltpu.VMEM((SEQ, LOCAL_HEADS, 3, TOKENS, HEAD_DIM), jnp.bfloat16),
            pltpu.VMEM((LOCAL_HEADS, LEN, LEN), jnp.bfloat16),
            pltpu.SemaphoreType.DMA((LOCAL_HEADS, 3)),
        ],
        compiler_params=pltpu.CompilerParams(vmem_limit_bytes=28 * MIB),
        cost_estimate=pl.CostEstimate(
            flops=4 * 2 * LOCAL_HEADS * LEN * LEN * HEAD_DIM,
            bytes_accessed=8 * MIB,
            transcendentals=0,
        ),
        name="attend_backward",
    )(heads, weights, out, grad_out)


def exchange(tensor, axis, size, bits):
    return lax.ppermute(tensor, axis, [(i, i ^ bits) for i in range(size)])


def total_over_depth(vector):
    moved = [exchange(vector, "seq", SEQ, bits) for bits in (2, 4, 6)]
    return (vector + moved[0]) + (moved[1] + moved[2])


def total_over_rest(vector):
    for axis, size, bit in (
        ("dp", DP, 1),
        ("dp", DP, 2),
        ("dp", DP, 4),
        ("dp", DP, 8),
        ("seq", SEQ, 1),
    ):
        vector = vector + exchange(vector, axis, size, bit)
    return vector


def shift_depth(tensor, steps):
    return lax.ppermute(tensor, "seq", [(i, (i + 2 * steps) % SEQ) for i in range(SEQ)])


def swap_cores(tensor):
    return exchange(tensor, "seq", SEQ, 1)


def after(tensors, *earlier):
    return lax.optimization_barrier((tensors, earlier))[0]


def per_device(qkv, cotangent, w_proj, clip_levels):
    place = lax.axis_index("seq")
    place_vector = place.astype(jnp.int32).reshape(1)
    clip = clip_levels.reshape(1, D)
    own = cotangent[0]
    own_rows = lax.optimization_barrier(
        lax.dynamic_slice_in_dim(w_proj, place * CHANNELS, CHANNELS, axis=0)
    )
    send = qkv[0].reshape(3, TOKENS, SEQ, LOCAL_HEADS, HEAD_DIM).transpose(2, 3, 0, 1, 4)
    heads = lax.all_to_all(send, "seq", split_axis=0, concat_axis=0, tiled=True)
    weight_max = jnp.max(jnp.abs(own_rows), axis=1).astype(jnp.float32)
    weight_max = weight_max.reshape(LOCAL_HEADS, 1, 128)
    own_swapped = swap_cores(own)
    own_1, weight_max = after((own, weight_max), heads)
    before = shift_depth(own_1, 1)
    behind = shift_depth(own_1, -1)
    weights, out, message = forward(heads, weight_max)
    is_bound = lax.broadcasted_iota(jnp.int32, message.shape, 0) == 2
    for bit in (1, 2, 4):
        message = jnp.maximum(message, exchange(message, "dp", DP, bit))
    before, behind = after((before, behind), message)
    halves, message = lax.optimization_barrier(((before[:HALF], behind[HALF:]), message))
    far_low = shift_depth(halves[0], 1)
    far_high = shift_depth(halves[1], -1)
    moved = [exchange(message, "seq", SEQ, bits) for bits in (2, 4, 6)]
    bound = jnp.maximum(jnp.maximum(message, moved[0]), jnp.maximum(moved[1], moved[2]))
    message = jnp.where(is_bound, bound, message)
    for bit in (8,):
        message = jnp.maximum(message, exchange(message, "dp", DP, bit))
    far_low, far_high, message = lax.optimization_barrier((far_low, far_high, message))
    pair = jnp.maximum(message, exchange(message, "seq", SEQ, 1))
    message = jnp.where(is_bound, pair, message)
    pieces = [own, before, behind, far_low, far_high, own_swapped]
    pieces += [swap_cores(piece) for piece in (before, behind, far_low, far_high)]
    grad_out, vector = projection(place_vector, message, message, weight_max, clip, out, own_rows, pieces)
    back = backward(heads, weights, out, grad_out)
    back, vector = lax.optimization_barrier((back, total_over_depth(vector)))
    received = lax.all_to_all(back, "seq", split_axis=0, concat_axis=0, tiled=True)
    vector = total_over_rest(vector)[0]
    grad_qkv = received.transpose(2, 3, 0, 1, 4).reshape(1, 3, TOKENS, HEADS, HEAD_DIM)
    return (grad_qkv, vector[: HEADS * HEAD_DIM], vector[HEADS * HEAD_DIM :])


def solution(mesh):
    in_specs = (P("dp", None, "seq", None, None), P("dp", "seq", None), P(), P())
    out_specs = (P("dp", None, "seq", None, None), P(), P())
    return jax.shard_map(
        per_device, mesh=mesh, in_specs=in_specs, out_specs=out_specs, check_vma=False
    )
```
